128 devices in a mesh: tile: 32 (over z, x, core), group: 4 (over y).
Axes of the slice: x: 4, y: 4, z: 4, core: 2. Of those that a mesh axis runs over, the one named last changes fastest.
Arguments:
- features: bfloat16 [4, 2048, 32, 256], P('group', 'tile'), may hold values from -6 to 6
- out_grad: bfloat16 [4, 704, 14, 14, 256], P('group', 'tile'), may hold values from -6 to 6
- pair_count: int32 [4, 32, 32], P('group'), may hold values from 0 to 2, as said below
- sample_grid: int32 [4, 32, 32, 2, 4, 14], P('group', 'tile'), may hold values from 0 to 62, as said below
- first_kernel: bfloat16 [3, 3, 256, 256], replicated, may hold values from -0.125 to 0.125
- second_kernel: bfloat16 [3, 3, 256, 256], replicated, may hold values from -0.125 to 0.125
Outputs:
- feature_grad: bfloat16 [4, 2048, 32, 256], P('group', 'tile')
- first_grad: float32 [3, 3, 256, 256], replicated
- second_grad: float32 [3, 3, 256, 256], replicated
The draws below stay inside these ranges and needn't reach their ends.
Inputs may be any that keep to these rules, and one draw needn't show every extreme that they name: Every entry is at most 2; in every scene each reader t has pair_count entries summing to exactly 22 over the owners, and every reader has some owner sending it exactly 2 regions. `sample_grid`: lower row indices are at most 62 and lower column indices at most 30; fractions lie in 0 to 15; along a slot's samples the positions (16 * lower index + fraction) ascend with a constant step of 8 to 64.
All inputs are finite; a program needn't handle non-finite values.
Results may differ from the reference program's by a relative error of at most 0.015.
Values may be sent and summed in bfloat16 or wider, within the bound.
A program may use at most 256 MiB of HBM per device.

```python
import math
import jax
import jax.numpy as jnp
from jax import lax

C = 256
RES = 14
TH = 64
TW = 32
CAP = 2
R_DEV = 22
SCENES = 4
READS = 704
ROWS = 2048
N_TILE = 32


def draw_pair_count(key, part):
    doubled = max(1, R_DEV // 4, R_DEV - N_TILE)
    chosen_count = R_DEV - doubled

    def one_scene(scene_key):
        heat_key, noise_key = jax.random.split(scene_key)
        heat_level = jax.random.randint(heat_key, (N_TILE,), 0, 4)
        noise_draw = jax.random.randint(noise_key, (N_TILE, N_TILE), 0, 1048576)
        owners = jnp.arange(N_TILE, dtype=jnp.int32)
        owner_score = (noise_draw + heat_level[None, :] * 524288) * 128 + owners[None, :]
        owner_rank = jnp.sum((owner_score[:, None, :] > owner_score[:, :, None]).astype(jnp.int32), axis=2)
        counts = (owner_rank < chosen_count).astype(jnp.int32) + (owner_rank < doubled).astype(jnp.int32)
        return counts.T
    return jax.vmap(one_scene)(jax.random.split(key, SCENES))


def draw_sample_grid(key, part):
    base_shape = (SCENES, N_TILE, N_TILE, CAP)
    steps_along = jnp.arange(RES, dtype=jnp.int32)

    def one_axis(axis_key, extent):
        step_key, start_key = jax.random.split(axis_key)
        stride_top = min(64, ((extent - 1) * 16 - 1) // (RES - 1))
        stride = jax.random.randint(step_key, base_shape, 8, stride_top + 1)
        anchor = jax.random.randint(start_key, base_shape, 0, (extent - 1) * 16 - (RES - 1) * stride)
        places = anchor[..., None] + stride[..., None] * steps_along
        return (places // 16, places % 16)
    row_key, col_key = jax.random.split(key)
    row_low, row_frac = one_axis(row_key, TH)
    col_low, col_frac = one_axis(col_key, TW)
    return jnp.stack([row_low, row_frac, col_low, col_frac], axis=-2).astype(jnp.int32)


def block_scale(own_key, shape, shards, low, high):
    level = 1.0
    for position, parts in shards:
        heights = jax.random.uniform(jax.random.fold_in(jax.random.fold_in(own_key, 6), position), (parts,), jnp.float32, low / len(shards), high / len(shards))
        level = level * jnp.repeat(jnp.exp(heights), shape[position] // parts).reshape((-1,) + (1,) * (len(shape) - 1 - position))
    return level


def noise(stream_key, shape, width, reach, cuts=(), kind=jnp.bfloat16):
    values = width * jax.random.normal(stream_key, shape, jnp.float32)
    if cuts:
        values = values * block_scale(stream_key, shape, cuts, -0.22, 0.18)
    return jnp.clip(values, -reach, reach).astype(kind)


def setup_inputs(seed: int = 0) -> dict:
    splits = jax.random.split(jax.random.key(seed), 7)
    features = noise(splits[0], (SCENES, ROWS, TW, C), 1.0, 6.0, ((0, 4), (1, 32)))
    out_grad = noise(splits[1], (SCENES, READS, RES, RES, C), 1.0, 6.0, ((0, 4), (1, 32)))
    pair_count = draw_pair_count(jax.random.fold_in(splits[6], 71), 0)
    sample_grid = draw_sample_grid(jax.random.fold_in(splits[6], 71), 0)
    first_kernel = noise(splits[4], (3, 3, C, C), (9 * C) ** -0.5, 0.125)
    second_kernel = noise(splits[5], (3, 3, C, C), (9 * C) ** -0.5, 0.125)
    return dict(features=features, out_grad=out_grad, pair_count=pair_count, sample_grid=sample_grid, first_kernel=first_kernel, second_kernel=second_kernel)


def interp_weights(lower_index, fraction, extent):
    places = jnp.arange(extent, dtype=jnp.int32)
    upper_share = fraction.astype(jnp.float32) / 16.0
    lower_part = jnp.where(places == lower_index[..., None], 1.0 - upper_share[..., None], 0.0)
    upper_part = jnp.where(places == lower_index[..., None] + 1, upper_share[..., None], 0.0)
    return lower_part + upper_part

def slot_weights(slot_grid, active, height, across):
    row_weights = interp_weights(slot_grid[..., 0, :], slot_grid[..., 1, :], height)
    row_weights = row_weights * active[..., None, None].astype(jnp.float32)
    col_weights = interp_weights(slot_grid[..., 2, :], slot_grid[..., 3, :], across)
    return (row_weights.astype(jnp.bfloat16), col_weights.astype(jnp.bfloat16))

def sample_blocks(tile_image, row_weights, col_weights):
    leading = row_weights.shape[:2]
    slot_total = leading[0] * leading[1]
    extent = row_weights.shape[2]
    row_blocks = row_weights.reshape(slot_total // 8, 8, extent, row_weights.shape[3])
    col_blocks = col_weights.reshape(slot_total // 8, 8, extent, col_weights.shape[3])
    image_wide = tile_image.astype(jnp.float32)

    def one_block(members):
        row_part, col_part = members
        stripes = jnp.einsum('spy,yxc->spxc', row_part.astype(jnp.float32), image_wide).astype(jnp.bfloat16)
        return jnp.einsum('sqx,spxc->spqc', col_part.astype(jnp.float32), stripes.astype(jnp.float32)).astype(jnp.bfloat16)
    sampled = lax.map(one_block, (row_blocks, col_blocks))
    return sampled.reshape(leading + (extent, extent, tile_image.shape[2]))

def spread_blocks(slot_grads, row_weights, col_weights):
    leading = row_weights.shape[:2]
    slot_total = leading[0] * leading[1]
    extent = row_weights.shape[2]
    height = row_weights.shape[3]
    across = col_weights.shape[3]
    channels = slot_grads.shape[-1]
    row_blocks = row_weights.reshape(slot_total // 8, 8, extent, height)
    col_blocks = col_weights.reshape(slot_total // 8, 8, extent, across)
    grad_blocks = slot_grads.reshape(slot_total // 8, 8, extent, extent, channels)

    def one_block(running_sum, members):
        row_part, col_part, grad_part = members
        stripes = jnp.einsum('sqx,spqc->spxc', col_part.astype(jnp.float32), grad_part.astype(jnp.float32)).astype(jnp.bfloat16)
        added = jnp.einsum('spy,spxc->yxc', row_part.astype(jnp.float32), stripes.astype(jnp.float32))
        return (running_sum + added, None)
    initial = jnp.zeros((height, across, channels), jnp.float32)
    summed, unused = lax.scan(one_block, initial, (row_blocks, col_blocks, grad_blocks))
    return summed.astype(jnp.bfloat16)

def unfold(values):
    region_count = values.shape[0]
    extent = values.shape[1]
    channels = values.shape[3]
    padded = jnp.pad(values, ((0, 0), (1, 1), (1, 1), (0, 0)))
    pieces = [padded[:, row_off:row_off + extent, col_off:col_off + extent, :] for row_off in range(3) for col_off in range(3)]
    return jnp.concatenate(pieces, axis=-1).reshape(region_count * extent * extent, 9 * channels)

def refold(columns, region_count, extent, channels):
    pieces = columns.reshape(region_count, extent, extent, 9, channels)
    padded = jnp.zeros((region_count, extent + 2, extent + 2, channels), columns.dtype)
    for row_off in range(3):
        for col_off in range(3):
            padded = padded.at[:, row_off:row_off + extent, col_off:col_off + extent, :].add(pieces[:, :, :, 3 * row_off + col_off, :])
    return padded[:, 1:-1, 1:-1, :]

def silu_slope(values):
    sigma = jax.nn.sigmoid(values)
    return sigma * (1.0 + values * (1.0 - sigma))

def region_pass(inputs, upstream, first_kernel, second_kernel):
    region_count = inputs.shape[0]
    extent = inputs.shape[1]
    channels = inputs.shape[3]
    first_flat = first_kernel.reshape(9 * channels, channels)
    second_flat = second_kernel.reshape(9 * channels, channels)
    input_cols = unfold(inputs)
    first_pre = jnp.dot(input_cols, first_flat, preferred_element_type=jnp.float32)
    hidden = jax.nn.silu(first_pre).astype(jnp.bfloat16)
    hidden_cols = unfold(hidden.reshape(region_count, extent, extent, channels))
    second_pre = jnp.dot(hidden_cols, second_flat, preferred_element_type=jnp.float32)
    second_delta = (upstream.reshape(-1, channels).astype(jnp.float32) * silu_slope(second_pre)).astype(jnp.bfloat16)
    second_raw = jnp.dot(hidden_cols.T, second_delta, preferred_element_type=jnp.float32)
    hidden_back = refold(jnp.dot(second_delta, second_flat.T, preferred_element_type=jnp.float32), region_count, extent, channels)
    first_delta = (hidden_back.reshape(-1, channels) * silu_slope(first_pre)).astype(jnp.bfloat16)
    first_raw = jnp.dot(input_cols.T, first_delta, preferred_element_type=jnp.float32)
    input_back = refold(jnp.dot(first_delta, first_flat.T, preferred_element_type=jnp.float32), region_count, extent, channels).astype(jnp.bfloat16)
    return (input_back, first_raw, second_raw)

def compact_plan(active, region_total):
    live_flags = active.reshape(-1)
    running = jnp.cumsum(live_flags.astype(jnp.int32), dtype=jnp.int32)
    region_ids = jnp.arange(region_total, dtype=jnp.int32)
    chosen = lax.optimization_barrier(jnp.sum((running[None, :] <= region_ids[:, None]).astype(jnp.int32), axis=1, dtype=jnp.int32))
    placed = jnp.maximum(running - 1, 0).astype(jnp.int32)
    return (chosen, placed, live_flags)

def scene_pass(scene_image, scene_upstream, counts, scene_grid, first_kernel, second_kernel):
    tile_images = scene_image.reshape(N_TILE, TH, TW, C)
    slot_ids = jnp.arange(CAP, dtype=jnp.int32)
    active = slot_ids[None, None, :] < counts[:, :, None]

    def owner_sample(members):
        owner_image, owner_grid, owner_active = members
        row_weights, col_weights = slot_weights(owner_grid, owner_active, TH, TW)
        return sample_blocks(owner_image, row_weights, col_weights)
    sent_blocks = lax.map(owner_sample, (tile_images, scene_grid, active))
    arrived = jnp.swapaxes(sent_blocks, 0, 1)
    reader_active = jnp.swapaxes(active, 0, 1)
    reader_upstream = scene_upstream.reshape(N_TILE, R_DEV, RES, RES, C)

    def reader_step(totals, members):
        reader_blocks, active_here, upstream_here = members
        chosen, placed, live_flags = compact_plan(active_here, R_DEV)
        inputs = jnp.take(reader_blocks.reshape(N_TILE * CAP, RES, RES, C), chosen, axis=0)
        input_back, first_raw, second_raw = region_pass(inputs, upstream_here, first_kernel, second_kernel)
        taken_back = jnp.take(input_back, placed, axis=0)
        slot_back = jnp.where(live_flags[:, None, None, None], taken_back, jnp.zeros_like(taken_back))
        return ((totals[0] + first_raw, totals[1] + second_raw), slot_back.reshape(N_TILE, CAP, RES, RES, C))
    zero_grad = jnp.zeros((9 * C, C), jnp.float32)
    sums, returned = lax.scan(reader_step, (zero_grad, zero_grad), (arrived, reader_active, reader_upstream))
    owner_back = jnp.swapaxes(returned, 0, 1)

    def owner_spread(members):
        owner_grads, owner_grid, owner_active = members
        row_weights, col_weights = slot_weights(owner_grid, owner_active, TH, TW)
        return spread_blocks(owner_grads, row_weights, col_weights)
    image_grads = lax.map(owner_spread, (owner_back, scene_grid, active))
    return (image_grads.reshape(N_TILE * TH, TW, C), sums[0], sums[1])

def reference(features, out_grad, pair_count, sample_grid, first_kernel, second_kernel):

    def one_scene(members):
        return scene_pass(members[0], members[1], members[2], members[3], first_kernel, second_kernel)
    image_grads, first_parts, second_parts = lax.map(one_scene, (features, out_grad, pair_count, sample_grid))
    grad_scale = 1.0 / math.sqrt(SCENES * N_TILE * R_DEV * RES * RES)
    first_grad = (lax.optimization_barrier(jnp.sum(first_parts, axis=0)) * grad_scale).reshape(3, 3, C, C)
    second_grad = (lax.optimization_barrier(jnp.sum(second_parts, axis=0)) * grad_scale).reshape(3, 3, C, C)
    return (image_grads, first_grad, second_grad)
```

```python
import functools
import math

import jax
import jax.numpy as jnp
from jax import lax
from jax.experimental import pallas as pl
from jax.experimental.pallas import tpu as pltpu
from jax.sharding import PartitionSpec as P

BF = jnp.bfloat16
F32 = jnp.float32
MESH = pl.DeviceIdType.MESH
RES = 14
PITCH = 16
FLAT = RES * PITCH
PACK = 200
CH = 256
WIDE = 3 * CH
TH = 64
TW = 32
VMEM = 60 * 1024 * 1024


def iota(shape, dim):
    return lax.broadcasted_iota(jnp.int32, shape, dim)


def dot(a, b):
    return jnp.dot(a, b, preferred_element_type=F32)


def packed_place(col):
    return jnp.where((col & 15) < RES, (col >> 4) * RES + (col & 15), -1)


def pack_kernel(place_ref, grad_ref, out_ref, padded, packed, sems):
    regions = grad_ref.shape[0]
    padded[...] = jnp.zeros_like(padded)
    perm = (iota((PACK, FLAT), 0) == packed_place(iota((PACK, FLAT), 1))).astype(F32).astype(BF)
    copies = []
    for k in range(regions):
        padded[k % 2, :, 0:RES, :] = grad_ref[k]
        flat = padded[k % 2].reshape(FLAT, CH)
        packed[k] = dot(perm, flat).astype(BF)
        copy = pltpu.make_async_copy(packed.at[k], out_ref.at[place_ref[k]], sems.at[k])
        copy.start()
        copies.append(copy)
    for copy in copies:
        copy.wait()


def pack_upstream(place, upstream, slots):
    regions = upstream.shape[0]
    return pl.pallas_call(
        pack_kernel,
        grid_spec=pltpu.PrefetchScalarGridSpec(
            num_scalar_prefetch=1,
            grid=(1,),
            in_specs=[pl.BlockSpec(upstream.shape, lambda i, p: (0, 0, 0, 0))],
            out_specs=pl.BlockSpec(memory_space=pl.ANY),
            scratch_shapes=[
                pltpu.VMEM((2, RES, PITCH, CH), BF),
                pltpu.VMEM((regions, PACK, CH), BF),
                pltpu.SemaphoreType.DMA((regions,)),
            ],
        ),
        out_shape=jax.ShapeDtypeStruct((slots, PACK, CH), BF),
        compiler_params=pltpu.CompilerParams(vmem_limit_bytes=VMEM),
    )(place, upstream)


def put_shifted(ref, r, value):
    ref[r, PITCH : PITCH + FLAT, 0:CH] = pltpu.roll(value, 1, 0).astype(BF)
    ref[r, PITCH : PITCH + FLAT, CH : 2 * CH] = value.astype(BF)
    ref[r, PITCH : PITCH + FLAT, 2 * CH : WIDE] = pltpu.roll(value, FLAT - 1, 0).astype(BF)


def clear_edges(ref):
    edge = jnp.zeros((ref.shape[0], PITCH, WIDE), BF)
    ref[:, 0:PITCH, :] = edge
    ref[:, PITCH + FLAT : 2 * PITCH + FLAT, :] = edge


def conv(ref, r, kernel_ref):
    total = dot(ref[r, 0:FLAT, :], kernel_ref[0])
    total += dot(ref[r, PITCH : PITCH + FLAT, :], kernel_ref[1])
    total += dot(ref[r, 2 * PITCH : 2 * PITCH + FLAT, :], kernel_ref[2])
    return total


def sampled_block(geo_ref, slot, tile_ref):
    row0, row_step = geo_ref[slot * 4], geo_ref[slot * 4 + 1]
    col0, col_step = geo_ref[slot * 4 + 2], geo_ref[slot * 4 + 3]
    lane, sub = iota((PITCH, CH), 1), iota((PITCH, CH), 0)
    reach = 16 - jnp.abs(16 * (lane & 31) - (col0 + col_step * sub))
    col_weight = jnp.where(sub < RES, jnp.maximum(reach, 0), 0).astype(F32)
    lower = (lane & 32) == 0
    owner = lane >> 6
    pieces = []
    for first in range(0, RES, 4):
        members = range(first, min(first + 4, RES))
        weights, rows = [], []
        for p in members:
            place = row0 + row_step * p
            low = place >> 4
            share = (place & 15).astype(F32) * (1.0 / 256.0)
            row_weight = jnp.where(lower, 1.0 / 16.0 - share, share)
            weights.append(jnp.where(owner == p - first, row_weight * col_weight, 0.0).astype(BF))
            rows.append(tile_ref[pl.ds(low, 2)].reshape(2 * TW, CH))
        depth = 64 * len(rows)
        left = jnp.concatenate(weights, axis=0)[:, 0:depth]
        pieces.append(dot(left, jnp.concatenate(rows, axis=0)))
    return jnp.concatenate(pieces, axis=0)


def sigmoid(v):
    return 0.5 * jnp.tanh(0.5 * v) + 0.5


def forward_kernel(steps_ref, *refs):
    wide_in, wide_hid = refs[-2:]

    @pl.when(pl.program_id(0) == 0)
    def _():
        clear_edges(wide_in)
        clear_edges(wide_hid)

    pl.when(pl.program_id(0) < steps_ref[0])(functools.partial(forward_step, *refs))


def forward_step(list_ref, geo_ref, tile_ref, first_ref, second_ref, out_ref, wide_in, wide_hid):
    step = pl.program_id(0)
    per = out_ref.shape[0]
    inside = (iota((FLAT, CH), 0) & 15) < RES
    for r in range(per):
        slot = list_ref[step * per + r]
        block = sampled_block(geo_ref, slot, tile_ref)
        put_shifted(wide_in, r, block)
        out_ref[r, 0] = block.astype(BF)
    for r in range(per):
        pre = conv(wide_in, r, first_ref)
        gate = sigmoid(pre)
        hidden = jnp.where(inside, pre * gate, 0.0)
        put_shifted(wide_hid, r, hidden)
        out_ref[r, 1] = hidden.astype(BF)
        out_ref[r, 2] = jnp.where(inside, gate * (1.0 + pre * (1.0 - gate)), 0.0).astype(BF)
    for r in range(per):
        pre = conv(wide_hid, r, second_ref)
        gate = sigmoid(pre)
        out_ref[r, 3] = (gate * (1.0 + pre * (1.0 - gate))).astype(BF)


PER = 2


def held(step, steps_ref):
    return jnp.minimum(step, steps_ref[0] - 1)


def forward(steps, slots, geo, tile, first, second):
    count = slots.shape[0]
    whole = lambda *shape: pl.BlockSpec(shape, lambda i, *_: (0,) * len(shape))
    return pl.pallas_call(
        forward_kernel,
        grid_spec=pltpu.PrefetchScalarGridSpec(
            num_scalar_prefetch=3,
            grid=(count // PER,),
            in_specs=[whole(TH, TW, CH), whole(3, WIDE, CH), whole(3, WIDE, CH)],
            out_specs=pl.BlockSpec(
                (PER, 4, FLAT, CH), lambda i, n, *_: (held(i, n), 0, 0, 0)
            ),
            scratch_shapes=[
                pltpu.VMEM((PER, FLAT + 2 * PITCH, WIDE), BF),
                pltpu.VMEM((PER, FLAT + 2 * PITCH, WIDE), BF),
            ],
        ),
        out_shape=jax.ShapeDtypeStruct((count, 4, FLAT, CH), BF),
        compiler_params=pltpu.CompilerParams(vmem_limit_bytes=VMEM),
    )(steps, slots, geo, tile, first, second)


def spread(geo_ref, slot, back, grad_ref):
    row0, row_step = geo_ref[slot * 4], geo_ref[slot * 4 + 1]
    col0, col_step = geo_ref[slot * 4 + 2], geo_ref[slot * 4 + 3]
    up, along = iota((CH, 128), 0), iota((CH, 128), 1)
    reach = 16 - jnp.abs(16 * (up & 31) - (col0 + col_step * (along & 15)))
    live = ((along & 15) < RES) & ((up >> 5) == (along >> 4))
    weight = jnp.where(live, jnp.maximum(reach, 0), 0).astype(F32) * (1.0 / 16.0)
    weight = weight.astype(BF)
    for first in (0, 8):
        members = min(8, RES - first)
        stripes = dot(
            weight[0 : members * TW, 0 : members * PITCH],
            back[first * PITCH : (first + members) * PITCH],
        )
        for k in range(members):
            place = row0 + row_step * (first + k)
            low = place >> 4
            share = (place & 15).astype(F32) * (1.0 / 16.0)
            stripe = stripes[k * TW : (k + 1) * TW]
            grad_ref[low] = grad_ref[low] + (1.0 - share) * stripe
            grad_ref[low + 1] = grad_ref[low + 1] + share * stripe


def backward_kernel(
    steps_ref, list_ref, live_ref, geo_ref, kept_ref, up_a, up_b, first_ref, second_ref,
    tile_out, first_out, second_out,
    wide_two, wide_one, first_acc, second_acc, tile_acc, *, scale
):
    step = pl.program_id(0)

    @pl.when(step == 0)
    def _():
        clear_edges(wide_two)
        clear_edges(wide_one)
        first_acc[...] = jnp.zeros_like(first_acc)
        second_acc[...] = jnp.zeros_like(second_acc)
        tile_acc[...] = jnp.zeros_like(tile_acc)

    @pl.when(step < steps_ref[0])
    def _():
        backward_step(
            list_ref, live_ref, geo_ref, kept_ref, up_a, up_b, first_ref, second_ref,
            wide_two, wide_one, first_acc, second_acc, tile_acc,
        )

    @pl.when(step == pl.num_programs(0) - 1)
    def _():
        tile_out[...] = tile_acc[...].astype(BF)
        for a in range(3):
            for b in range(3):
                cols = slice((2 - b) * CH, (3 - b) * CH)
                first_out[a, b] = (first_acc[2 - a, :, cols] * scale).astype(first_out.dtype)
                second_out[a, b] = (second_acc[2 - a, :, cols] * scale).astype(second_out.dtype)


def backward_step(
    list_ref, live_ref, geo_ref, kept_ref, up_a, up_b, first_ref, second_ref,
    wide_two, wide_one, first_acc, second_acc, tile_acc
):
    step = pl.program_id(0)
    per = kept_ref.shape[0]
    unpack = (iota((FLAT, PACK), 1) == packed_place(iota((FLAT, PACK), 0))).astype(F32).astype(BF)
    across_rows = (((0,), (0,)), ((), ()))
    for r, up in enumerate((up_a, up_b)):
        live = live_ref[step * per + r] > 0
        packed = jnp.where(live, up[0], jnp.zeros_like(up[0]))
        put_shifted(wide_two, r, dot(unpack, packed) * kept_ref[r, 3].astype(F32))
    for a in range(3):
        for r in range(per):
            second_acc[a] += lax.dot_general(
                kept_ref[r, 1], wide_two[r, PITCH * a : PITCH * a + FLAT, :],
                across_rows, preferred_element_type=F32,
            )
    for r in range(per):
        put_shifted(wide_one, r, conv(wide_two, r, second_ref) * kept_ref[r, 2].astype(F32))
    for a in range(3):
        for r in range(per):
            first_acc[a] += lax.dot_general(
                kept_ref[r, 0], wide_one[r, PITCH * a : PITCH * a + FLAT, :],
                across_rows, preferred_element_type=F32,
            )
    for r in range(per):
        back = conv(wide_one, r, first_ref).astype(BF)
        spread(geo_ref, list_ref[step * per + r], back, tile_acc)


def backward(steps, slots, live, geo, kept, arrived, first_back, second_back, scale):
    whole = lambda *shape: pl.BlockSpec(shape, lambda i, *_: (0,) * len(shape))
    kernel_shape = jax.ShapeDtypeStruct((3, 3, CH, CH), BF)
    return pl.pallas_call(
        functools.partial(backward_kernel, scale=scale),
        grid_spec=pltpu.PrefetchScalarGridSpec(
            num_scalar_prefetch=4,
            grid=(slots.shape[0] // PER,),
            in_specs=[
                pl.BlockSpec((PER, 4, FLAT, CH), lambda i, n, *_: (held(i, n), 0, 0, 0)),
                pl.BlockSpec((1, PACK, CH), lambda i, n, s, *_: (s[PER * held(i, n)], 0, 0)),
                pl.BlockSpec((1, PACK, CH), lambda i, n, s, *_: (s[PER * held(i, n) + 1], 0, 0)),
                whole(3, WIDE, CH),
                whole(3, WIDE, CH),
            ],
            out_specs=[whole(TH, TW, CH), whole(3, 3, CH, CH), whole(3, 3, CH, CH)],
            scratch_shapes=[
                pltpu.VMEM((PER, FLAT + 2 * PITCH, WIDE), BF),
                pltpu.VMEM((PER, FLAT + 2 * PITCH, WIDE), BF),
                pltpu.VMEM((3, CH, WIDE), F32),
                pltpu.VMEM((3, CH, WIDE), F32),
                pltpu.VMEM((TH, TW, CH), F32),
            ],
        ),
        out_shape=[jax.ShapeDtypeStruct((TH, TW, CH), BF), kernel_shape, kernel_shape],
        compiler_params=pltpu.CompilerParams(vmem_limit_bytes=VMEM),
    )(steps, slots, live, geo, kept, arrived, arrived, first_back, second_back)


def reduce_kernel(planes, lines, mine_ref, out_ref, pair_in, half, shards, line_in, total, sems_s, sems_r):
    tile, line = lax.axis_index("tile"), lax.axis_index("group")
    core, chip = tile & 1, tile >> 1
    rows = mine_ref.shape[1]
    share = rows // planes
    other = (tile + 1) - 2 * core

    def plane_peer(k):
        return 2 * lax.rem(chip + k, planes) + core

    def line_peer(k):
        return lax.rem(line + k, lines)

    barrier = pltpu.get_barrier_semaphore()
    pl.semaphore_signal(barrier, inc=1, device_id={"tile": other}, device_id_type=MESH)

    def greet_plane(k, carry):
        pl.semaphore_signal(barrier, inc=1, device_id={"tile": plane_peer(k)}, device_id_type=MESH)
        return carry

    lax.fori_loop(1, planes, greet_plane, 0)
    for k in range(1, lines):
        pl.semaphore_signal(barrier, inc=1, device_id={"group": line_peer(k)}, device_id_type=MESH)
    pl.semaphore_wait(barrier, 1 + (planes - 1) + (lines - 1))

    swap = pltpu.make_async_remote_copy(
        mine_ref.at[1 - core], pair_in, sems_s.at[0], sems_r.at[0],
        device_id={"tile": other}, device_id_type=MESH,
    )
    swap.start()
    swap.wait()

    def add_pair(k, carry):
        at = pl.ds(pl.multiple_of(k * share, 16), share)
        half[at] = (mine_ref[core, at].astype(F32) + pair_in[at].astype(F32)).astype(BF)
        return carry

    lax.fori_loop(0, planes, add_pair, 0)

    def scatter(k):
        to = lax.rem(chip + k, planes)
        return pltpu.make_async_remote_copy(
            half.at[pl.ds(pl.multiple_of(to * share, 16), share)], shards.at[k - 1],
            sems_s.at[k], sems_r.at[k], device_id={"tile": 2 * to + core}, device_id_type=MESH,
        )

    def start_scatter(k, carry):
        scatter(k).start()
        return carry

    def wait_scatter(k, carry):
        scatter(k).wait()
        return carry

    lax.fori_loop(1, planes, start_scatter, 0)
    lax.fori_loop(1, planes, wait_scatter, 0)
    here = pl.ds(pl.multiple_of(chip * share, 16), share)
    partial = half[here].astype(F32)
    for k in range(planes - 1):
        partial += shards[k].astype(F32)
    total[...] = partial.astype(BF)

    moves = []
    for k in range(1, lines):
        move = pltpu.make_async_remote_copy(
            total, line_in.at[k - 1], sems_s.at[planes + k], sems_r.at[planes + k],
            device_id={"group": line_peer(k)}, device_id_type=MESH,
        )
        move.start()
        moves.append(move)
    for move in moves:
        move.wait()
    terms = [total[...].astype(F32)] + [line_in[k].astype(F32) for k in range(lines - 1)]
    final = None
    for position in range(lines):
        term = terms[0]
        for k in range(1, lines):
            term = jnp.where(lax.rem(line + lines - k, lines) == position, terms[k], term)
        final = term if final is None else final + term
    out_ref[core, here] = final.astype(BF)

    def gather(k, origin):
        at = pl.ds(pl.multiple_of(origin * share, 16), share)
        return pltpu.make_async_remote_copy(
            out_ref.at[core, at], out_ref.at[core, at],
            sems_s.at[planes + lines + k], sems_r.at[planes + lines + k],
            device_id={"tile": plane_peer(k)}, device_id_type=MESH,
        )

    def start_gather(k, carry):
        gather(k, chip).start()
        return carry

    def wait_gather(k, carry):
        gather(k, chip).wait_send()
        gather(k, lax.rem(chip - k + planes, planes)).wait_recv()
        return carry

    lax.fori_loop(1, planes, start_gather, 0)
    lax.fori_loop(1, planes, wait_gather, 0)

    last = pltpu.make_async_remote_copy(
        out_ref.at[core], out_ref.at[core], sems_s.at[planes], sems_r.at[planes],
        device_id={"tile": other}, device_id_type=MESH,
    )
    last.start()
    last.wait_send()
    pltpu.make_async_remote_copy(
        out_ref.at[1 - core], out_ref.at[1 - core], sems_s.at[planes], sems_r.at[planes],
        device_id={"tile": other}, device_id_type=MESH,
    ).wait_recv()


def reduce_everywhere(mine, tiles, lines):
    planes = tiles // 2
    rows = mine.shape[1]
    share = rows // planes
    spec = pl.BlockSpec(memory_space=pltpu.VMEM)
    return pl.pallas_call(
        functools.partial(reduce_kernel, planes, lines),
        in_specs=[spec],
        out_specs=spec,
        out_shape=jax.ShapeDtypeStruct(mine.shape, BF),
        scratch_shapes=[
            pltpu.VMEM((rows, CH), BF),
            pltpu.VMEM((rows, CH), BF),
            pltpu.VMEM((planes - 1, share, CH), BF),
            pltpu.VMEM((lines - 1, share, CH), BF),
            pltpu.VMEM((share, CH), BF),
            pltpu.SemaphoreType.DMA((2 * planes + lines,)),
            pltpu.SemaphoreType.DMA((2 * planes + lines,)),
        ],
        compiler_params=pltpu.CompilerParams(
            collective_id=0, has_side_effects=True, vmem_limit_bytes=VMEM
        ),
    )(mine)


def turned(kernel):
    return jnp.transpose(kernel[::-1, ::-1], (0, 1, 3, 2)).reshape(3, WIDE, CH)


def send_plan(column, regions):
    owners = column.shape[0]
    ids = jnp.arange(owners, dtype=jnp.int32)
    before = jnp.sum(jnp.where(ids[None, :] < ids[:, None], column[None, :], 0), axis=1)
    k = jnp.arange(regions, dtype=jnp.int32)[:, None]
    mine = (before[None, :] <= k) & (k < (before + column)[None, :])
    spot = (k - before[None, :]) * owners + ids[None, :]
    return jnp.sum(jnp.where(mine, spot, 0), axis=1, dtype=jnp.int32)


def work_plan(row, per):
    readers = row.shape[0]
    ids = jnp.arange(readers, dtype=jnp.int32)
    place = jnp.arange(2 * readers, dtype=jnp.int32)[:, None]
    start = jnp.int32(0)
    slots = jnp.zeros((2 * readers,), jnp.int32)
    live = jnp.zeros((2 * readers,), jnp.int32)
    for s in range(2):
        has = row > s
        rank = jnp.sum(jnp.where((ids[None, :] < ids[:, None]) & has[None, :], 1, 0), axis=1)
        hit = has[None, :] & (start + rank[None, :] == place)
        slots += jnp.sum(jnp.where(hit, s * readers + ids[None, :], 0), axis=1, dtype=jnp.int32)
        live += jnp.sum(hit, axis=1, dtype=jnp.int32)
        start = start + (jnp.sum(has, dtype=jnp.int32) + per - 1) // per * per
    return slots, live, jnp.maximum(start // per, 1).reshape(1)


def on_device(features, out_grad, pair_count, sample_grid, first_kernel, second_kernel):
    tiles, lines = lax.axis_size("tile"), lax.axis_size("group")
    own = lax.axis_index("tile")
    counts = pair_count[0]
    upstream = out_grad[0]
    regions = upstream.shape[0]
    column = lax.dynamic_index_in_dim(counts, own, 1, keepdims=False)
    row = lax.dynamic_index_in_dim(counts, own, 0, keepdims=False)

    packed = pack_upstream(send_plan(column, regions), upstream, 2 * tiles)
    packed = packed.reshape(2, tiles, PACK, CH)
    arrived = lax.all_to_all(packed, "tile", split_axis=1, concat_axis=1, tiled=True)
    arrived = arrived.reshape(2 * tiles, PACK, CH)

    grid = jnp.swapaxes(sample_grid[0, 0], 0, 1).reshape(2 * tiles, 4, RES)
    row_at = 16 * grid[:, 0, 0:2] + grid[:, 1, 0:2]
    col_at = 16 * grid[:, 2, 0:2] + grid[:, 3, 0:2]
    geo = jnp.stack(
        [row_at[:, 0], row_at[:, 1] - row_at[:, 0], col_at[:, 0], col_at[:, 1] - col_at[:, 0]],
        axis=1,
    ).reshape(-1)
    slots, live, steps = work_plan(row, PER)
    kept = forward(
        steps, slots, geo, features[0],
        first_kernel.reshape(3, WIDE, CH), second_kernel.reshape(3, WIDE, CH),
    )
    scale = 1.0 / math.sqrt(lines * tiles * regions * RES * RES)
    tile_grad, first_part, second_part = backward(
        steps, slots, live, geo, kept, arrived, turned(first_kernel), turned(second_kernel), scale
    )
    parts = jnp.stack([first_part.reshape(9 * CH, CH), second_part.reshape(9 * CH, CH)])
    sums = reduce_everywhere(parts, tiles, lines).astype(F32).reshape(2, 3, 3, CH, CH)
    return tile_grad[None], sums[0], sums[1]


def solution(mesh):
    return jax.shard_map(
        on_device,
        mesh=mesh,
        in_specs=(
            P("group", "tile", None, None),
            P("group", "tile", None, None, None),
            P("group", None, None),
            P("group", "tile", None, None, None, None),
            P(),
            P(),
        ),
        out_specs=(P("group", "tile", None, None), P(), P()),
        check_vma=False,
    )
```

```python
import functools
import math

import jax
import jax.numpy as jnp
from jax import lax
from jax.experimental import pallas as pl
from jax.experimental.pallas import tpu as pltpu
from jax.sharding import PartitionSpec as P

BF = jnp.bfloat16
F32 = jnp.float32
MESH = pl.DeviceIdType.MESH
RES = 14
PITCH = 16
FLAT = RES * PITCH
PACK = 200
CH = 256
WIDE = 3 * CH
TH = 64
TW = 32
VMEM = 60 * 1024 * 1024


def iota(shape, dim):
    return lax.broadcasted_iota(jnp.int32, shape, dim)


def dot(a, b):
    return jnp.dot(a, b, preferred_element_type=F32)


def packed_place(col):
    return jnp.where((col & 15) < RES, (col >> 4) * RES + (col & 15), -1)


def pack_kernel(slot_ref, owner_ref, grad_ref, out_zero, out_one, padded, packed, sems):
    regions = grad_ref.shape[0]
    padded[...] = jnp.zeros_like(padded)
    perm = (iota((PACK, FLAT), 0) == packed_place(iota((PACK, FLAT), 1))).astype(F32).astype(BF)

    def copy(k, out_ref):
        return pltpu.make_async_copy(packed.at[k], out_ref.at[owner_ref[k]], sems.at[k])

    for k in range(regions):
        padded[k % 4, :, 0:RES, :] = grad_ref[k]
        packed[k] = dot(perm, padded[k % 4].reshape(FLAT, CH)).astype(BF)
        for s, out_ref in enumerate((out_zero, out_one)):
            pl.when(slot_ref[k] == s)(copy(k, out_ref).start)
    for k in range(regions):
        copy(k, out_zero).wait()


def pack_upstream(plan, upstream, owners):
    regions = upstream.shape[0]
    return pl.pallas_call(
        pack_kernel,
        grid_spec=pltpu.PrefetchScalarGridSpec(
            num_scalar_prefetch=2,
            grid=(1,),
            in_specs=[pl.BlockSpec(upstream.shape, lambda i, *_: (0, 0, 0, 0))],
            out_specs=[pl.BlockSpec(memory_space=pl.ANY)] * 2,
            scratch_shapes=[
                pltpu.VMEM((4, RES, PITCH, CH), BF),
                pltpu.VMEM((regions, PACK, CH), BF),
                pltpu.SemaphoreType.DMA((regions,)),
            ],
        ),
        out_shape=[jax.ShapeDtypeStruct((owners, PACK, CH), BF)] * 2,
        compiler_params=pltpu.CompilerParams(vmem_limit_bytes=VMEM),
    )(*plan, upstream)


def put_shifted(ref, r, value):
    ref[r, PITCH : PITCH + FLAT, 0:CH] = pltpu.roll(value, 1, 0).astype(BF)
    ref[r, PITCH : PITCH + FLAT, CH : 2 * CH] = value.astype(BF)
    ref[r, PITCH : PITCH + FLAT, 2 * CH : WIDE] = pltpu.roll(value, FLAT - 1, 0).astype(BF)


def clear_edges(ref):
    edge = jnp.zeros((ref.shape[0], PITCH, WIDE), BF)
    ref[:, 0:PITCH, :] = edge
    ref[:, PITCH + FLAT : 2 * PITCH + FLAT, :] = edge


def taps(ref, r):
    return jnp.concatenate([ref[r, PITCH * a : PITCH * a + FLAT, :] for a in range(3)], axis=1)


def conv(ref, r, kernel_ref):
    return dot(taps(ref, r), kernel_ref[...].reshape(9 * CH, CH))


def conv_back(ref, r, kernel_ref):
    turned = jnp.concatenate([kernel_ref[8 - n] for n in range(9)], axis=1)
    return lax.dot_general(
        taps(ref, r), turned, (((1,), (1,)), ((), ())), preferred_element_type=F32
    )


def sampled_block(geo_ref, slot, tile_ref):
    row0, row_step = geo_ref[slot * 4], geo_ref[slot * 4 + 1]
    col0, col_step = geo_ref[slot * 4 + 2], geo_ref[slot * 4 + 3]
    lane, sub = iota((PITCH, CH), 1), iota((PITCH, CH), 0)
    reach = 16 - jnp.abs(16 * (lane & 31) - (col0 + col_step * sub))
    col_weight = jnp.where(sub < RES, jnp.maximum(reach, 0), 0).astype(F32)
    lower = (lane & 32) == 0
    owner = lane >> 6
    pieces = []
    for first in range(0, RES, 4):
        members = range(first, min(first + 4, RES))
        weights, rows = [], []
        for p in members:
            place = row0 + row_step * p
            low = place >> 4
            share = (place & 15).astype(F32) * (1.0 / 256.0)
            row_weight = jnp.where(lower, 1.0 / 16.0 - share, share)
            weights.append(jnp.where(owner == p - first, row_weight * col_weight, 0.0).astype(BF))
            rows.append(tile_ref[pl.ds(low, 2)].reshape(2 * TW, CH))
        depth = 64 * len(rows)
        left = jnp.concatenate(weights, axis=0)[:, 0:depth]
        pieces.append(dot(left, jnp.concatenate(rows, axis=0)))
    return jnp.concatenate(pieces, axis=0)


def sigmoid(v):
    return 0.5 * jnp.tanh(0.5 * v) + 0.5


def forward_kernel(steps_ref, *refs):
    wide_in, wide_hid = refs[-2:]

    @pl.when(pl.program_id(0) == 0)
    def _():
        clear_edges(wide_in)
        clear_edges(wide_hid)

    pl.when(pl.program_id(0) < steps_ref[0])(functools.partial(forward_step, *refs))


def forward_step(list_ref, geo_ref, tile_ref, first_ref, second_ref, out_ref, wide_in, wide_hid):
    step = pl.program_id(0)
    per = out_ref.shape[0]
    inside = (iota((FLAT, CH), 0) & 15) < RES
    for r in range(per):
        slot = list_ref[step * per + r]
        block = sampled_block(geo_ref, slot, tile_ref)
        put_shifted(wide_in, r, block)
        out_ref[r, 0] = block.astype(BF)
    for r in range(per):
        pre = conv(wide_in, r, first_ref)
        gate = sigmoid(pre)
        hidden = jnp.where(inside, pre * gate, 0.0)
        put_shifted(wide_hid, r, hidden)
        out_ref[r, 1] = hidden.astype(BF)
        out_ref[r, 2] = jnp.where(inside, gate * (1.0 + pre * (1.0 - gate)), 0.0).astype(BF)
    for r in range(per):
        pre = conv(wide_hid, r, second_ref)
        gate = sigmoid(pre)
        out_ref[r, 3] = (gate * (1.0 + pre * (1.0 - gate))).astype(BF)


PER = 4


def held(step, steps_ref):
    return jnp.minimum(step, steps_ref[0] - 1)


def forward(steps, slots, geo, tile, first, second):
    count = slots.shape[0]
    whole = lambda *shape: pl.BlockSpec(shape, lambda i, *_: (0,) * len(shape))
    return pl.pallas_call(
        forward_kernel,
        grid_spec=pltpu.PrefetchScalarGridSpec(
            num_scalar_prefetch=3,
            grid=(count // PER,),
            in_specs=[whole(TH, TW, CH), whole(9, CH, CH), whole(9, CH, CH)],
            out_specs=pl.BlockSpec(
                (PER, 4, FLAT, CH), lambda i, n, *_: (held(i, n), 0, 0, 0)
            ),
            scratch_shapes=[
                pltpu.VMEM((PER, FLAT + 2 * PITCH, WIDE), BF),
                pltpu.VMEM((PER, FLAT + 2 * PITCH, WIDE), BF),
            ],
        ),
        out_shape=jax.ShapeDtypeStruct((count, 4, FLAT, CH), BF),
        compiler_params=pltpu.CompilerParams(vmem_limit_bytes=VMEM),
    )(steps, slots, geo, tile, first, second)


def spread(geo_ref, slots, backs, grad_ref):
    up, along = iota((CH, 128), 0), iota((CH, 128), 1)
    same = ((along & 15) < RES) & ((up >> 5) == (along >> 4))
    weights = []
    for slot in slots:
        col0, col_step = geo_ref[slot * 4 + 2], geo_ref[slot * 4 + 3]
        reach = 16 - jnp.abs(16 * (up & 31) - (col0 + col_step * (along & 15)))
        weight = jnp.where(same, jnp.maximum(reach, 0), 0).astype(F32) * (1.0 / 16.0)
        weights.append(weight.astype(BF))
    for first in (0, 8):
        members = min(8, RES - first)
        stripes = [
            dot(
                weight[0 : members * TW, 0 : members * PITCH],
                back[first * PITCH : (first + members) * PITCH],
            )
            for weight, back in zip(weights, backs)
        ]
        for k in range(members):
            for slot, each in zip(slots, stripes):
                place = geo_ref[slot * 4] + geo_ref[slot * 4 + 1] * (first + k)
                low = place >> 4
                share = (place & 15).astype(F32) * (1.0 / 16.0)
                stripe = each[k * TW : (k + 1) * TW]
                upper = share * stripe
                pair = jnp.concatenate([(stripe - upper)[None], upper[None]], axis=0)
                grad_ref[pl.ds(low, 2)] = grad_ref[pl.ds(low, 2)] + pair


def backward_step(at, list_ref, live_ref, geo_ref, kept_ref, ups, first_ref, second_ref, scratch):
    wide_two, wide_one, first_acc, second_acc, tile_acc = scratch
    per = kept_ref.shape[0]
    unpack = (iota((FLAT, PACK), 1) == packed_place(iota((FLAT, PACK), 0))).astype(F32).astype(BF)
    for r, up in enumerate(ups):
        packed = jnp.where(live_ref[at + r] > 0, up[0], jnp.zeros_like(up[0]))
        put_shifted(wide_two, r, dot(unpack, packed) * kept_ref[r, 3].astype(F32))
    kernel_sums(kept_ref, 1, wide_two, second_acc)
    for r in range(per):
        hidden_back = conv_back(wide_two, r, second_ref)
        put_shifted(wide_one, r, hidden_back * kept_ref[r, 2].astype(F32))
    kernel_sums(kept_ref, 0, wide_one, first_acc)
    backs = [conv_back(wide_one, r, first_ref).astype(BF) for r in range(per)]
    spread(geo_ref, [list_ref[at + r] for r in range(per)], backs, tile_acc)


def kernel_sums(kept_ref, which, wide, acc):
    per = kept_ref.shape[0]
    values = kept_ref[:, which].reshape(per * FLAT, CH)
    for a in range(3):
        acc[a] += lax.dot_general(
            values, wide[:, PITCH * a : PITCH * a + FLAT, :].reshape(per * FLAT, WIDE),
            (((0,), (0,)), ((), ())), preferred_element_type=F32,
        )


def backward_kernel(begun, scale, steps_ref, list_ref, live_ref, geo_ref, kept_ref, *refs):
    ups, refs = refs[:PER], refs[PER:]
    first_ref, second_ref, refs = refs[0], refs[1], refs[2:]
    sums, refs = (refs[:3], refs[3:]) if begun else (None, refs)
    scratch = refs[-5:] if begun else refs[3:5] + refs[:3]
    wide_two, wide_one, first_acc, second_acc, tile_acc = scratch
    step = pl.program_id(0)

    @pl.when(step == 0)
    def _():
        clear_edges(wide_two)
        clear_edges(wide_one)
        first_acc[...] = jnp.zeros_like(first_acc)
        second_acc[...] = jnp.zeros_like(second_acc)
        tile_acc[...] = jnp.zeros_like(tile_acc)

    @pl.when(step < steps_ref[0])
    def _():
        at = (steps_ref[1] + step) * PER
        backward_step(at, list_ref, live_ref, geo_ref, kept_ref, ups, first_ref, second_ref, scratch)

    if begun:

        @pl.when(step == pl.num_programs(0) - 1)
        def _():
            tile_out, kernels_out = refs[:2]
            tile_out[...] = (tile_acc[...] + sums[2][...]).astype(BF)
            for n in range(9):
                row, cols = (8 - n) // 3, slice((8 - n) % 3 * CH, ((8 - n) % 3 + 1) * CH)
                for w, acc in enumerate((first_acc, second_acc)):
                    total = acc[row, :, cols] + sums[w][row, :, cols]
                    kernels_out[w, n * CH : (n + 1) * CH] = (total * scale).astype(BF)


def backward(slot, plan, geo, kept, arrived, first, second, sums, scale):
    steps, slots, live = plan
    readers = arrived.shape[0]
    begun = sums is not None
    whole = lambda *shape: pl.BlockSpec(shape, lambda i, *_: (0,) * len(shape))
    last = slots.shape[0] // PER - 1

    def group(i, n):
        return jnp.clip(n[1] + jnp.minimum(i, n[0] - 1), 0, last)

    def from_reader(j):
        def block(i, n, s, *_):
            return jnp.clip(s[PER * group(i, n) + j] - slot * readers, 0, readers - 1), 0, 0

        return pl.BlockSpec((1, PACK, CH), block)

    totals = [(3, CH, WIDE), (3, CH, WIDE), (TH, TW, CH)]
    wide = [pltpu.VMEM((PER, FLAT + 2 * PITCH, WIDE), BF)] * 2
    if begun:
        outs = [jax.ShapeDtypeStruct((TH, TW, CH), BF), jax.ShapeDtypeStruct((2, 9 * CH, CH), BF)]
        scratch = wide + [pltpu.VMEM(t, F32) for t in totals]
    else:
        outs = [jax.ShapeDtypeStruct(t, F32) for t in totals]
        scratch = wide
    return pl.pallas_call(
        functools.partial(backward_kernel, begun, scale),
        grid_spec=pltpu.PrefetchScalarGridSpec(
            num_scalar_prefetch=4,
            grid=(readers // PER,),
            in_specs=[
                pl.BlockSpec((PER, 4, FLAT, CH), lambda i, n, *_: (group(i, n), 0, 0, 0)),
                *[from_reader(j) for j in range(PER)],
                whole(9, CH, CH),
                whole(9, CH, CH),
                *([whole(*t) for t in totals] if begun else []),
            ],
            out_specs=[whole(*o.shape) for o in outs],
            scratch_shapes=scratch,
        ),
        out_shape=outs,
        compiler_params=pltpu.CompilerParams(vmem_limit_bytes=VMEM),
    )(steps, slots, live, geo, kept, *[arrived] * PER, first, second, *(sums or ()))


SIDE = 4
ORDERS = ((0, 1, 2), (1, 2, 0), (2, 0, 1))


def reduce_kernel(mine_ref, out_ref, pair_in, half, in_one, held_one, in_two, held_two, in_three, sems_s, sems_r):
    tile, line = lax.axis_index("tile"), lax.axis_index("group")
    core, x, z = tile & 1, (tile >> 1) & 3, tile >> 3
    coords = (z, x, line)
    third = mine_ref.shape[1] // 3
    quarter, small = third // SIDE, third // SIDE // SIDE

    def peer(axis, k):
        to = (coords[axis] + k) & (SIDE - 1)
        if axis == 0:
            return {"tile": to * 8 + x * 2 + core}
        if axis == 1:
            return {"tile": z * 8 + to * 2 + core}
        return {"group": to}

    other = {"tile": tile + 1 - 2 * core}

    def rows(start, size):
        return pl.ds(pl.multiple_of(start, 16), size)

    def remote(source, target, sem, device):
        return pltpu.make_async_remote_copy(
            source, target, sems_s.at[sem], sems_r.at[sem], device_id=device, device_id_type=MESH
        )

    barrier = pltpu.get_barrier_semaphore()
    pl.semaphore_signal(barrier, inc=1, device_id=other, device_id_type=MESH)
    for axis in range(3):
        for k in range(1, SIDE):
            pl.semaphore_signal(barrier, inc=1, device_id=peer(axis, k), device_id_type=MESH)
    pl.semaphore_wait(barrier, 1 + 3 * (SIDE - 1))

    def sem(stage, part, k):
        return 6 + (stage * 3 + part) * 3 + k - 1

    def swap(part):
        at = slice(part * third, (part + 1) * third)
        return remote(mine_ref.at[1 - core, at], pair_in.at[at], part, other)

    def one(part, k):
        axis = ORDERS[part][0]
        to = (coords[axis] + k) & (SIDE - 1)
        source = half.at[rows(part * third + to * quarter, quarter)]
        return remote(source, in_one.at[part, k - 1], sem(0, part, k), peer(axis, k))

    def two(part, k):
        axis = ORDERS[part][1]
        to = (coords[axis] + k) & (SIDE - 1)
        source = held_one.at[part, rows(to * small, small)]
        return remote(source, in_two.at[part, k - 1], sem(1, part, k), peer(axis, k))

    def three(part, k):
        return remote(held_two.at[part], in_three.at[part, k - 1], sem(2, part, k), peer(ORDERS[part][2], k))

    def start_of(part, first, second):
        return part * third + first * quarter + second * small

    def back_two(part, k, sender):
        first, second = ORDERS[part][:2]
        at = rows(start_of(part, coords[first], sender), small)
        return remote(out_ref.at[core, at], out_ref.at[core, at], sem(3, part, k), peer(second, k))

    def back_one(part, k, sender):
        first = ORDERS[part][0]
        at = rows(part * third + sender * quarter, quarter)
        return remote(out_ref.at[core, at], out_ref.at[core, at], sem(4, part, k), peer(first, k))

    def give(part, of):
        at = slice(part * third, (part + 1) * third)
        return remote(out_ref.at[of, at], out_ref.at[of, at], 3 + part, other)

    shifts = range(1, SIDE)
    parts = range(3)
    for part in parts:
        swap(part).start()
    for part in parts:
        swap(part).wait()
        at = slice(part * third, (part + 1) * third)
        half[at] = (mine_ref[core, at].astype(F32) + pair_in[at].astype(F32)).astype(BF)
        for k in shifts:
            one(part, k).start()
    for part in parts:
        own = coords[ORDERS[part][0]]
        total = half[rows(part * third + own * quarter, quarter)].astype(F32)
        for k in shifts:
            one(part, k).wait()
            total += in_one[part, k - 1].astype(F32)
        held_one[part] = total.astype(BF)
        for k in shifts:
            two(part, k).start()
    for part in parts:
        own = coords[ORDERS[part][1]]
        total = held_one[part, rows(own * small, small)].astype(F32)
        for k in shifts:
            two(part, k).wait()
            total += in_two[part, k - 1].astype(F32)
        held_two[part] = total.astype(BF)
        for k in shifts:
            three(part, k).start()
    for part in parts:
        first, second, axis = ORDERS[part]
        terms = [held_two[part].astype(F32)]
        for k in shifts:
            three(part, k).wait()
            terms.append(in_three[part, k - 1].astype(F32))
        total = None
        for place in range(SIDE):
            back = (coords[axis] - place) & (SIDE - 1)
            term = terms[0]
            for k in shifts:
                term = jnp.where(back == k, terms[k], term)
            total = term if total is None else total + term
        out_ref[core, rows(start_of(part, coords[first], coords[second]), small)] = total.astype(BF)
        for k in shifts:
            back_two(part, k, coords[second]).start()
    for part in parts:
        first, second, axis = ORDERS[part]
        for k in shifts:
            back_two(part, k, coords[second]).wait_send()
            back_two(part, k, (coords[second] - k) & (SIDE - 1)).wait_recv()
        for k in shifts:
            back_one(part, k, coords[first]).start()
    for part in parts:
        first = ORDERS[part][0]
        for k in shifts:
            back_one(part, k, coords[first]).wait_send()
            back_one(part, k, (coords[first] - k) & (SIDE - 1)).wait_recv()
        give(part, core).start()
    for part in parts:
        give(part, core).wait_send()
        give(part, 1 - core).wait_recv()


def reduce_everywhere(mine):
    rows = mine.shape[1]
    third = rows // 3
    quarter, small = third // SIDE, third // SIDE // SIDE
    spec = pl.BlockSpec(memory_space=pltpu.VMEM)
    return pl.pallas_call(
        reduce_kernel,
        in_specs=[spec],
        out_specs=spec,
        out_shape=jax.ShapeDtypeStruct(mine.shape, BF),
        scratch_shapes=[
            pltpu.VMEM((rows, CH), BF),
            pltpu.VMEM((rows, CH), BF),
            pltpu.VMEM((3, SIDE - 1, quarter, CH), BF),
            pltpu.VMEM((3, quarter, CH), BF),
            pltpu.VMEM((3, SIDE - 1, small, CH), BF),
            pltpu.VMEM((3, small, CH), BF),
            pltpu.VMEM((3, SIDE - 1, small, CH), BF),
            pltpu.SemaphoreType.DMA((6 + 45,)),
            pltpu.SemaphoreType.DMA((6 + 45,)),
        ],
        compiler_params=pltpu.CompilerParams(
            collective_id=0, has_side_effects=True, vmem_limit_bytes=VMEM
        ),
    )(mine)


def send_plan(column, regions):
    owners = column.shape[0]
    ids = jnp.arange(owners, dtype=jnp.int32)
    before = jnp.sum(jnp.where(ids[None, :] < ids[:, None], column[None, :], 0), axis=1)
    k = jnp.arange(regions, dtype=jnp.int32)[:, None]
    mine = (before[None, :] <= k) & (k < (before + column)[None, :])
    slot = jnp.sum(jnp.where(mine, k - before[None, :], 0), axis=1, dtype=jnp.int32)
    owner = jnp.sum(jnp.where(mine, ids[None, :], 0), axis=1, dtype=jnp.int32)
    return slot, owner


def work_plan(row):
    readers = row.shape[0]
    ids = jnp.arange(readers, dtype=jnp.int32)
    place = jnp.arange(2 * readers, dtype=jnp.int32)[:, None]
    steps_zero = (jnp.sum(row > 0, dtype=jnp.int32) + PER - 1) // PER
    steps_one = (jnp.sum(row > 1, dtype=jnp.int32) + PER - 1) // PER
    slots, live = 0, 0
    for s, start in ((0, 0), (1, PER * steps_zero)):
        has = row > s
        rank = jnp.sum(jnp.where((ids[None, :] < ids[:, None]) & has[None, :], 1, 0), axis=1)
        hit = has[None, :] & (start + rank[None, :] == place)
        slots += jnp.sum(jnp.where(hit, s * readers + ids[None, :], 0), axis=1, dtype=jnp.int32)
        live += jnp.sum(hit, axis=1, dtype=jnp.int32)
    zero = jnp.stack([steps_zero, jnp.zeros_like(steps_zero)])
    one = jnp.stack([steps_one, steps_zero])
    return slots, live, jnp.maximum(steps_zero + steps_one, 1).reshape(1), zero, one


def exchange(blocks):
    return lax.all_to_all(blocks, "tile", split_axis=0, concat_axis=0, tiled=True)


def on_device(features, out_grad, pair_count, sample_grid, first_kernel, second_kernel):
    tiles, lines = lax.axis_size("tile"), lax.axis_size("group")
    own = lax.axis_index("tile")
    counts = pair_count[0]
    upstream = out_grad[0]
    regions = upstream.shape[0]
    column = lax.dynamic_index_in_dim(counts, own, 1, keepdims=False)
    row = lax.dynamic_index_in_dim(counts, own, 0, keepdims=False)

    packed = pack_upstream(send_plan(column, regions), upstream, tiles)
    arrived = [exchange(packed[0])]

    grid = jnp.swapaxes(sample_grid[0, 0], 0, 1).reshape(2 * tiles, 4, RES)
    row_at = 16 * grid[:, 0, 0:2] + grid[:, 1, 0:2]
    col_at = 16 * grid[:, 2, 0:2] + grid[:, 3, 0:2]
    geo = jnp.stack(
        [row_at[:, 0], row_at[:, 1] - row_at[:, 0], col_at[:, 0], col_at[:, 1] - col_at[:, 0]],
        axis=1,
    ).reshape(-1)
    slots, live, steps, zero, one = work_plan(row)
    first, second = first_kernel.reshape(9, CH, CH), second_kernel.reshape(9, CH, CH)
    kept = forward(steps, slots, geo, features[0], first, second)
    later, kept = lax.optimization_barrier((packed[1], kept))
    arrived.append(exchange(later))
    scale = 1.0 / math.sqrt(lines * tiles * regions * RES * RES)
    sums = backward(0, (zero, slots, live), geo, kept, arrived[0], first, second, None, scale)
    tile_grad, parts = backward(1, (one, slots, live), geo, kept, arrived[1], first, second, sums, scale)
    totals = reduce_everywhere(parts).astype(F32).reshape(2, 3, 3, CH, CH)
    return tile_grad[None], totals[0], totals[1]


def solution(mesh):
    return jax.shard_map(
        on_device,
        mesh=mesh,
        in_specs=(
            P("group", "tile", None, None),
            P("group", "tile", None, None, None),
            P("group", None, None),
            P("group", "tile", None, None, None, None),
            P(),
            P(),
        ),
        out_specs=(P("group", "tile", None, None), P(), P()),
        check_vma=False,
    )
```

```python
import functools
import math

import jax
import jax.numpy as jnp
from jax import lax
from jax.experimental import pallas as pl
from jax.experimental.pallas import tpu as pltpu
from jax.sharding import PartitionSpec as P

BF = jnp.bfloat16
F32 = jnp.float32
MESH = pl.DeviceIdType.MESH
RES = 14
PITCH = 16
FLAT = RES * PITCH
PACK = 200
CH = 256
WIDE = 3 * CH
TH = 64
TW = 32
VMEM = 60 * 1024 * 1024


def iota(shape, dim):
    return lax.broadcasted_iota(jnp.int32, shape, dim)


def dot(a, b):
    return jnp.dot(a, b, preferred_element_type=F32)


def packed_place(col):
    return jnp.where((col & 15) < RES, (col >> 4) * RES + (col & 15), -1)


def pack_kernel(slot_ref, owner_ref, grad_ref, out_zero, out_one, padded, packed, sems):
    regions = grad_ref.shape[0]
    padded[...] = jnp.zeros_like(padded)
    perm = (iota((PACK, FLAT), 0) == packed_place(iota((PACK, FLAT), 1))).astype(F32).astype(BF)

    def copy(k, out_ref):
        return pltpu.make_async_copy(packed.at[k], out_ref.at[owner_ref[k]], sems.at[k])

    for k in range(regions):
        padded[k % 4, :, 0:RES, :] = grad_ref[k]
        packed[k] = dot(perm, padded[k % 4].reshape(FLAT, CH)).astype(BF)
        for s, out_ref in enumerate((out_zero, out_one)):
            pl.when(slot_ref[k] == s)(copy(k, out_ref).start)
    for k in range(regions):
        copy(k, out_zero).wait()


def pack_upstream(plan, upstream, owners):
    regions = upstream.shape[0]
    return pl.pallas_call(
        pack_kernel,
        grid_spec=pltpu.PrefetchScalarGridSpec(
            num_scalar_prefetch=2,
            grid=(1,),
            in_specs=[pl.BlockSpec(upstream.shape, lambda i, *_: (0, 0, 0, 0))],
            out_specs=[pl.BlockSpec(memory_space=pl.ANY)] * 2,
            scratch_shapes=[
                pltpu.VMEM((4, RES, PITCH, CH), BF),
                pltpu.VMEM((regions, PACK, CH), BF),
                pltpu.SemaphoreType.DMA((regions,)),
            ],
        ),
        out_shape=[jax.ShapeDtypeStruct((owners, PACK, CH), BF)] * 2,
        compiler_params=pltpu.CompilerParams(vmem_limit_bytes=VMEM),
    )(*plan, upstream)


def put_shifted(ref, r, value):
    ref[r, PITCH : PITCH + FLAT, 0:CH] = pltpu.roll(value, 1, 0).astype(BF)
    ref[r, PITCH : PITCH + FLAT, CH : 2 * CH] = value.astype(BF)
    ref[r, PITCH : PITCH + FLAT, 2 * CH : WIDE] = pltpu.roll(value, FLAT - 1, 0).astype(BF)


def clear_edges(ref):
    edge = jnp.zeros((ref.shape[0], PITCH, WIDE), BF)
    ref[:, 0:PITCH, :] = edge
    ref[:, PITCH + FLAT : 2 * PITCH + FLAT, :] = edge


def conv(ref, r, kernel_ref, a):
    return dot(ref[r, PITCH * a : PITCH * a + FLAT, :], kernel_ref[3 * a : 3 * a + 3].reshape(WIDE, CH))


def conv_back(ref, r, kernel_ref):
    sides = [ref[r, PITCH * a : PITCH * a + FLAT, :] for a in range(3)]
    return dot(jnp.concatenate(sides, axis=1), kernel_ref[...].reshape(9 * CH, CH))


def sampled_block(geo_ref, slot, tile_ref):
    row0, row_step = geo_ref[slot * 4], geo_ref[slot * 4 + 1]
    col0, col_step = geo_ref[slot * 4 + 2], geo_ref[slot * 4 + 3]
    lane, sub = iota((PITCH, CH), 1), iota((PITCH, CH), 0)
    reach = 16 - jnp.abs(16 * (lane & 31) - (col0 + col_step * sub))
    col_weight = jnp.where(sub < RES, jnp.maximum(reach, 0), 0).astype(F32)
    lower = (lane & 32) == 0
    owner = lane >> 6
    pieces = []
    for first in range(0, RES, 4):
        members = range(first, min(first + 4, RES))
        weights, rows = [], []
        for p in members:
            place = row0 + row_step * p
            low = place >> 4
            share = (place & 15).astype(F32) * (1.0 / 256.0)
            row_weight = jnp.where(lower, 1.0 / 16.0 - share, share)
            weights.append(jnp.where(owner == p - first, row_weight * col_weight, 0.0).astype(BF))
            rows.append(tile_ref[pl.ds(low, 2)].reshape(2 * TW, CH))
        depth = 64 * len(rows)
        left = jnp.concatenate(weights, axis=0)[:, 0:depth]
        pieces.append(dot(left, jnp.concatenate(rows, axis=0)))
    return jnp.concatenate(pieces, axis=0)


def sigmoid(v):
    return 0.5 * jnp.tanh(0.5 * v) + 0.5


def forward_kernel(steps_ref, *refs):
    wide_in, wide_hid = refs[-2:]

    @pl.when(pl.program_id(0) == 0)
    def _():
        clear_edges(wide_in)
        clear_edges(wide_hid)

    pl.when(pl.program_id(0) < steps_ref[0])(functools.partial(forward_step, *refs))


def forward_step(list_ref, geo_ref, tile_ref, first_ref, second_ref, out_ref, wide_in, wide_hid):
    step = pl.program_id(0)
    per = out_ref.shape[0]
    inside = (iota((FLAT, CH), 0) & 15) < RES

    def sample(r):
        block = sampled_block(geo_ref, list_ref[step * per + r], tile_ref)
        put_shifted(wide_in, r, block)
        out_ref[r, 0] = block.astype(BF)

    def hide(r, pre):
        gate = sigmoid(pre)
        hidden = jnp.where(inside, pre * gate, 0.0)
        put_shifted(wide_hid, r, hidden)
        out_ref[r, 1] = hidden.astype(BF)
        out_ref[r, 2] = jnp.where(inside, gate + hidden * (1.0 - gate), 0.0).astype(BF)

    def finish(r, pre):
        gate = sigmoid(pre)
        out_ref[r, 3] = (gate * (1.0 + pre * (1.0 - gate))).astype(BF)

    sample(0)
    held_pre = None
    for r in range(per):
        pre = conv(wide_in, r, first_ref, 0)
        if r + 1 < per:
            sample(r + 1)
        pre += conv(wide_in, r, first_ref, 1)
        if r:
            hide(r - 1, held_pre)
        pre += conv(wide_in, r, first_ref, 2)
        held_pre = pre
    last = held_pre
    for r in range(per):
        pre = conv(wide_hid, r, second_ref, 0)
        if r == 0:
            hide(per - 1, last)
        else:
            finish(r - 1, held_pre)
        pre += conv(wide_hid, r, second_ref, 1)
        pre += conv(wide_hid, r, second_ref, 2)
        held_pre = pre
    finish(per - 1, held_pre)


PER = 4


def held(step, steps_ref):
    return jnp.minimum(step, steps_ref[0] - 1)


def forward(steps, slots, geo, tile, first, second):
    count = slots.shape[0]
    whole = lambda *shape: pl.BlockSpec(shape, lambda i, *_: (0,) * len(shape))
    return pl.pallas_call(
        forward_kernel,
        grid_spec=pltpu.PrefetchScalarGridSpec(
            num_scalar_prefetch=3,
            grid=(count // PER,),
            in_specs=[whole(TH, TW, CH), whole(9, CH, CH), whole(9, CH, CH)],
            out_specs=pl.BlockSpec(
                (PER, 4, FLAT, CH), lambda i, n, *_: (held(i, n), 0, 0, 0)
            ),
            scratch_shapes=[
                pltpu.VMEM((PER, FLAT + 2 * PITCH, WIDE), BF),
                pltpu.VMEM((PER, FLAT + 2 * PITCH, WIDE), BF),
            ],
        ),
        out_shape=jax.ShapeDtypeStruct((count, 4, FLAT, CH), BF),
        compiler_params=pltpu.CompilerParams(vmem_limit_bytes=VMEM),
    )(steps, slots, geo, tile, first, second)


def spread(geo_ref, slot, back, grad_ref, half):
    up, along = iota((CH, 128), 0), iota((CH, 128), 1)
    col0, col_step = geo_ref[slot * 4 + 2], geo_ref[slot * 4 + 3]
    same = ((along & 15) < RES) & ((up >> 5) == (along >> 4))
    reach = 16 - jnp.abs(16 * (up & 31) - (col0 + col_step * (along & 15)))
    weight = jnp.where(same, jnp.maximum(reach, 0), 0).astype(F32) * (1.0 / 16.0)
    first = 8 * half
    members = min(8, RES - first)
    stripes = dot(
        weight[0 : members * TW, 0 : members * PITCH].astype(BF),
        back[first * PITCH : (first + members) * PITCH],
    )
    for k in range(members):
        place = geo_ref[slot * 4] + geo_ref[slot * 4 + 1] * (first + k)
        low = place >> 4
        share = (place & 15).astype(F32) * (1.0 / 16.0)
        stripe = stripes[k * TW : (k + 1) * TW]
        upper = share * stripe
        pair = jnp.concatenate([(stripe - upper)[None], upper[None]], axis=0)
        grad_ref[pl.ds(low, 2)] = grad_ref[pl.ds(low, 2)] + pair


def backward_step(at, list_ref, live_ref, geo_ref, kept_ref, ups, first_ref, second_ref, scratch):
    wide_two, wide_one, first_acc, second_acc, tile_acc = scratch
    per = kept_ref.shape[0]
    unpack = (iota((FLAT, PACK), 1) == packed_place(iota((FLAT, PACK), 0))).astype(F32).astype(BF)
    def upstream(r):
        packed = jnp.where(live_ref[at + r] > 0, ups[r][0], jnp.zeros_like(ups[r][0]))
        put_shifted(wide_two, r, dot(unpack, packed) * kept_ref[r, 3].astype(F32))

    def first_delta(r, hidden_back):
        put_shifted(wide_one, r, hidden_back * kept_ref[r, 2].astype(F32))

    def give_back(r, back, half):
        spread(geo_ref, list_ref[at + r], back, tile_acc, half)

    upstream(0)
    upstream(1)
    held = []
    for r in range(per):
        held.append(conv_back(wide_two, r, second_ref))
        if r + 2 < per:
            upstream(r + 2)
        if r:
            first_delta(r - 1, held[r - 1])
    kernel_sums(kept_ref, 1, wide_two, second_acc, 0)
    first_delta(per - 1, held[per - 1])
    kernel_sums(kept_ref, 1, wide_two, second_acc, 1)
    kernel_sums(kept_ref, 1, wide_two, second_acc, 2)
    held = []
    for r in range(per):
        held.append(conv_back(wide_one, r, first_ref).astype(BF))
    for a in range(3):
        kernel_sums(kept_ref, 0, wide_one, first_acc, a)
        give_back(a, held[a], 0)
        give_back(a, held[a], 1)
    give_back(3, held[3], 0)
    give_back(3, held[3], 1)


def kernel_sums(kept_ref, which, wide, acc, a):
    per = kept_ref.shape[0]
    values = kept_ref[:, which].reshape(per * FLAT, CH)
    acc[a] += lax.dot_general(
        values, wide[:, PITCH * a : PITCH * a + FLAT, :].reshape(per * FLAT, WIDE),
        (((0,), (0,)), ((), ())), preferred_element_type=F32,
    )


def backward_kernel(begun, scale, steps_ref, list_ref, live_ref, geo_ref, kept_ref, *refs):
    ups, refs = refs[:PER], refs[PER:]
    first_ref, second_ref, refs = refs[0], refs[1], refs[2:]
    sums, refs = (refs[:3], refs[3:]) if begun else (None, refs)
    scratch = refs[-5:] if begun else refs[3:5] + refs[:3]
    wide_two, wide_one, first_acc, second_acc, tile_acc = scratch
    step = pl.program_id(0)

    @pl.when(step == 0)
    def _():
        clear_edges(wide_two)
        clear_edges(wide_one)
        first_acc[...] = jnp.zeros_like(first_acc)
        second_acc[...] = jnp.zeros_like(second_acc)
        tile_acc[...] = jnp.zeros_like(tile_acc)

    @pl.when(step < steps_ref[0])
    def _():
        at = (steps_ref[1] + step) * PER
        backward_step(at, list_ref, live_ref, geo_ref, kept_ref, ups, first_ref, second_ref, scratch)

    if begun:

        @pl.when(step == pl.num_programs(0) - 1)
        def _():
            tile_out, kernels_out = refs[:2]
            tile_out[...] = (tile_acc[...] + sums[2][...]).astype(BF)
            for n in range(9):
                row, cols = (8 - n) // 3, slice((8 - n) % 3 * CH, ((8 - n) % 3 + 1) * CH)
                for w, acc in enumerate((first_acc, second_acc)):
                    total = acc[row, :, cols] + sums[w][row, :, cols]
                    kernels_out[w, n * CH : (n + 1) * CH] = (total * scale).astype(BF)


def backward(slot, plan, geo, kept, arrived, first, second, sums, scale):
    steps, slots, live = plan
    readers = arrived.shape[0]
    begun = sums is not None
    whole = lambda *shape: pl.BlockSpec(shape, lambda i, *_: (0,) * len(shape))
    last = slots.shape[0] // PER - 1

    def group(i, n):
        return jnp.clip(n[1] + jnp.minimum(i, n[0] - 1), 0, last)

    def from_reader(j):
        def block(i, n, s, *_):
            return jnp.clip(s[PER * group(i, n) + j] - slot * readers, 0, readers - 1), 0, 0

        return pl.BlockSpec((1, PACK, CH), block)

    totals = [(3, CH, WIDE), (3, CH, WIDE), (TH, TW, CH)]
    wide = [pltpu.VMEM((PER, FLAT + 2 * PITCH, WIDE), BF)] * 2
    if begun:
        outs = [jax.ShapeDtypeStruct((TH, TW, CH), BF), jax.ShapeDtypeStruct((2, 9 * CH, CH), BF)]
        scratch = wide + [pltpu.VMEM(t, F32) for t in totals]
    else:
        outs = [jax.ShapeDtypeStruct(t, F32) for t in totals]
        scratch = wide
    return pl.pallas_call(
        functools.partial(backward_kernel, begun, scale),
        grid_spec=pltpu.PrefetchScalarGridSpec(
            num_scalar_prefetch=4,
            grid=(readers // PER,),
            in_specs=[
                pl.BlockSpec((PER, 4, FLAT, CH), lambda i, n, *_: (group(i, n), 0, 0, 0)),
                *[from_reader(j) for j in range(PER)],
                whole(9, CH, CH),
                whole(9, CH, CH),
                *([whole(*t) for t in totals] if begun else []),
            ],
            out_specs=[whole(*o.shape) for o in outs],
            scratch_shapes=scratch,
        ),
        out_shape=outs,
        compiler_params=pltpu.CompilerParams(vmem_limit_bytes=VMEM),
    )(steps, slots, live, geo, kept, *[arrived] * PER, first, second, *(sums or ()))


SIDE = 4
ORDERS = ((0, 1, 2), (1, 2, 0), (2, 0, 1))


def reduce_kernel(mine_ref, out_ref, pair_in, half, in_one, held_one, in_two, held_two, in_three, sems_s, sems_r):
    tile, line = lax.axis_index("tile"), lax.axis_index("group")
    core, x, z = tile & 1, (tile >> 1) & 3, tile >> 3
    coords = (z, x, line)
    third = mine_ref.shape[1] // 3
    quarter, small = third // SIDE, third // SIDE // SIDE

    def peer(axis, k):
        to = (coords[axis] + k) & (SIDE - 1)
        if axis == 0:
            return {"tile": to * 8 + x * 2 + core}
        if axis == 1:
            return {"tile": z * 8 + to * 2 + core}
        return {"group": to}

    other = {"tile": tile + 1 - 2 * core}

    def rows(start, size):
        return pl.ds(pl.multiple_of(start, 16), size)

    def remote(source, target, sem, device):
        return pltpu.make_async_remote_copy(
            source, target, sems_s.at[sem], sems_r.at[sem], device_id=device, device_id_type=MESH
        )

    barrier = pltpu.get_barrier_semaphore()
    pl.semaphore_signal(barrier, inc=1, device_id=other, device_id_type=MESH)
    for axis in range(3):
        for k in range(1, SIDE):
            pl.semaphore_signal(barrier, inc=1, device_id=peer(axis, k), device_id_type=MESH)
    pl.semaphore_wait(barrier, 1 + 3 * (SIDE - 1))

    def sem(stage, part, k):
        return 6 + (stage * 3 + part) * 3 + k - 1

    def swap(part):
        at = slice(part * third, (part + 1) * third)
        return remote(mine_ref.at[1 - core, at], pair_in.at[at], part, other)

    def one(part, k):
        axis = ORDERS[part][0]
        to = (coords[axis] + k) & (SIDE - 1)
        source = half.at[rows(part * third + to * quarter, quarter)]
        return remote(source, in_one.at[part, k - 1], sem(0, part, k), peer(axis, k))

    def two(part, k):
        axis = ORDERS[part][1]
        to = (coords[axis] + k) & (SIDE - 1)
        source = held_one.at[part, rows(to * small, small)]
        return remote(source, in_two.at[part, k - 1], sem(1, part, k), peer(axis, k))

    def three(part, k):
        return remote(held_two.at[part], in_three.at[part, k - 1], sem(2, part, k), peer(ORDERS[part][2], k))

    def start_of(part, first, second):
        return part * third + first * quarter + second * small

    def back_two(part, k, sender):
        first, second = ORDERS[part][:2]
        at = rows(start_of(part, coords[first], sender), small)
        return remote(out_ref.at[core, at], out_ref.at[core, at], sem(3, part, k), peer(second, k))

    def back_one(part, k, sender):
        first = ORDERS[part][0]
        at = rows(part * third + sender * quarter, quarter)
        return remote(out_ref.at[core, at], out_ref.at[core, at], sem(4, part, k), peer(first, k))

    def give(part, of):
        at = slice(part * third, (part + 1) * third)
        return remote(out_ref.at[of, at], out_ref.at[of, at], 3 + part, other)

    shifts = range(1, SIDE)
    parts = range(3)
    for part in parts:
        swap(part).start()
    for part in parts:
        swap(part).wait()
        at = slice(part * third, (part + 1) * third)
        half[at] = (mine_ref[core, at].astype(F32) + pair_in[at].astype(F32)).astype(BF)
        for k in shifts:
            one(part, k).start()
    for part in parts:
        own = coords[ORDERS[part][0]]
        total = half[rows(part * third + own * quarter, quarter)].astype(F32)
        for k in shifts:
            one(part, k).wait()
            total += in_one[part, k - 1].astype(F32)
        held_one[part] = total.astype(BF)
        for k in shifts:
            two(part, k).start()
    for part in parts:
        own = coords[ORDERS[part][1]]
        total = held_one[part, rows(own * small, small)].astype(F32)
        for k in shifts:
            two(part, k).wait()
            total += in_two[part, k - 1].astype(F32)
        held_two[part] = total.astype(BF)
        for k in shifts:
            three(part, k).start()
    for part in parts:
        first, second, axis = ORDERS[part]
        terms = [held_two[part].astype(F32)]
        for k in shifts:
            three(part, k).wait()
            terms.append(in_three[part, k - 1].astype(F32))
        total = None
        for place in range(SIDE):
            back = (coords[axis] - place) & (SIDE - 1)
            term = terms[0]
            for k in shifts:
                term = jnp.where(back == k, terms[k], term)
            total = term if total is None else total + term
        out_ref[core, rows(start_of(part, coords[first], coords[second]), small)] = total.astype(BF)
        for k in shifts:
            back_two(part, k, coords[second]).start()
    for part in parts:
        first, second, axis = ORDERS[part]
        for k in shifts:
            back_two(part, k, coords[second]).wait_send()
            back_two(part, k, (coords[second] - k) & (SIDE - 1)).wait_recv()
        for k in shifts:
            back_one(part, k, coords[first]).start()
    for part in parts:
        first = ORDERS[part][0]
        for k in shifts:
            back_one(part, k, coords[first]).wait_send()
            back_one(part, k, (coords[first] - k) & (SIDE - 1)).wait_recv()
        give(part, core).start()
    for part in parts:
        give(part, core).wait_send()
        give(part, 1 - core).wait_recv()


def reduce_everywhere(mine):
    rows = mine.shape[1]
    third = rows // 3
    quarter, small = third // SIDE, third // SIDE // SIDE
    spec = pl.BlockSpec(memory_space=pltpu.VMEM)
    return pl.pallas_call(
        reduce_kernel,
        in_specs=[spec],
        out_specs=spec,
        out_shape=jax.ShapeDtypeStruct(mine.shape, BF),
        scratch_shapes=[
            pltpu.VMEM((rows, CH), BF),
            pltpu.VMEM((rows, CH), BF),
            pltpu.VMEM((3, SIDE - 1, quarter, CH), BF),
            pltpu.VMEM((3, quarter, CH), BF),
            pltpu.VMEM((3, SIDE - 1, small, CH), BF),
            pltpu.VMEM((3, small, CH), BF),
            pltpu.VMEM((3, SIDE - 1, small, CH), BF),
            pltpu.SemaphoreType.DMA((6 + 45,)),
            pltpu.SemaphoreType.DMA((6 + 45,)),
        ],
        compiler_params=pltpu.CompilerParams(
            collective_id=0, has_side_effects=True, vmem_limit_bytes=VMEM
        ),
    )(mine)


def send_plan(column, regions):
    owners = column.shape[0]
    ids = jnp.arange(owners, dtype=jnp.int32)
    before = jnp.sum(jnp.where(ids[None, :] < ids[:, None], column[None, :], 0), axis=1)
    k = jnp.arange(regions, dtype=jnp.int32)[:, None]
    mine = (before[None, :] <= k) & (k < (before + column)[None, :])
    slot = jnp.sum(jnp.where(mine, k - before[None, :], 0), axis=1, dtype=jnp.int32)
    owner = jnp.sum(jnp.where(mine, ids[None, :], 0), axis=1, dtype=jnp.int32)
    return slot, owner


def work_plan(row):
    readers = row.shape[0]
    ids = jnp.arange(readers, dtype=jnp.int32)
    place = jnp.arange(2 * readers, dtype=jnp.int32)[:, None]
    steps_zero = (jnp.sum(row > 0, dtype=jnp.int32) + PER - 1) // PER
    steps_one = (jnp.sum(row > 1, dtype=jnp.int32) + PER - 1) // PER
    slots, live = 0, 0
    for s, start in ((0, 0), (1, PER * steps_zero)):
        has = row > s
        rank = jnp.sum(jnp.where((ids[None, :] < ids[:, None]) & has[None, :], 1, 0), axis=1)
        hit = has[None, :] & (start + rank[None, :] == place)
        slots += jnp.sum(jnp.where(hit, s * readers + ids[None, :], 0), axis=1, dtype=jnp.int32)
        live += jnp.sum(hit, axis=1, dtype=jnp.int32)
    zero = jnp.stack([steps_zero, jnp.zeros_like(steps_zero)])
    one = jnp.stack([steps_one, steps_zero])
    return slots, live, jnp.maximum(steps_zero + steps_one, 1).reshape(1), zero, one


def turned(kernel):
    return jnp.transpose(kernel[::-1, ::-1], (0, 1, 3, 2)).reshape(9, CH, CH)


def exchange(blocks):
    return lax.all_to_all(blocks, "tile", split_axis=0, concat_axis=0, tiled=True)


def on_device(features, out_grad, pair_count, sample_grid, first_kernel, second_kernel):
    tiles, lines = lax.axis_size("tile"), lax.axis_size("group")
    own = lax.axis_index("tile")
    counts = pair_count[0]
    upstream = out_grad[0]
    regions = upstream.shape[0]
    column = lax.dynamic_index_in_dim(counts, own, 1, keepdims=False)
    row = lax.dynamic_index_in_dim(counts, own, 0, keepdims=False)

    packed = pack_upstream(send_plan(column, regions), upstream, tiles)
    arrived = [exchange(packed[0])]

    grid = jnp.swapaxes(sample_grid[0, 0], 0, 1).reshape(2 * tiles, 4, RES)
    row_at = 16 * grid[:, 0, 0:2] + grid[:, 1, 0:2]
    col_at = 16 * grid[:, 2, 0:2] + grid[:, 3, 0:2]
    geo = jnp.stack(
        [row_at[:, 0], row_at[:, 1] - row_at[:, 0], col_at[:, 0], col_at[:, 1] - col_at[:, 0]],
        axis=1,
    ).reshape(-1)
    slots, live, steps, zero, one = work_plan(row)
    first, second = first_kernel.reshape(9, CH, CH), second_kernel.reshape(9, CH, CH)
    kept = forward(steps, slots, geo, features[0], first, second)
    later, kept = lax.optimization_barrier((packed[1], kept))
    arrived.append(exchange(later))
    first, second = turned(first_kernel), turned(second_kernel)
    scale = 1.0 / math.sqrt(lines * tiles * regions * RES * RES)
    sums = backward(0, (zero, slots, live), geo, kept, arrived[0], first, second, None, scale)
    tile_grad, parts = backward(1, (one, slots, live), geo, kept, arrived[1], first, second, sums, scale)
    totals = reduce_everywhere(parts).astype(F32).reshape(2, 3, 3, CH, CH)
    return tile_grad[None], totals[0], totals[1]


def solution(mesh):
    return jax.shard_map(
        on_device,
        mesh=mesh,
        in_specs=(
            P("group", "tile", None, None),
            P("group", "tile", None, None, None),
            P("group", None, None),
            P("group", "tile", None, None, None, None),
            P(),
            P(),
        ),
        out_specs=(P("group", "tile", None, None), P(), P()),
        check_vma=False,
    )
```

```python
import functools
import math

import jax
import jax.numpy as jnp
from jax import lax
from jax.experimental import pallas as pl
from jax.experimental.pallas import tpu as pltpu
from jax.sharding import PartitionSpec as P

BF = jnp.bfloat16
F32 = jnp.float32
MESH = pl.DeviceIdType.MESH
RES = 14
PITCH = 16
FLAT = RES * PITCH
PACK = 200
CH = 256
WIDE = 3 * CH
TH = 64
TW = 32
VMEM = 60 * 1024 * 1024


def iota(shape, dim):
    return lax.broadcasted_iota(jnp.int32, shape, dim)


def dot(a, b):
    return jnp.dot(a, b, preferred_element_type=F32)


def packed_place(col):
    return jnp.where((col & 15) < RES, (col >> 4) * RES + (col & 15), -1)


def pack_kernel(slot_ref, owner_ref, grad_ref, out_zero, out_one, padded, packed, sems):
    regions = grad_ref.shape[0]
    padded[...] = jnp.zeros_like(padded)
    perm = (iota((PACK, FLAT), 0) == packed_place(iota((PACK, FLAT), 1))).astype(F32).astype(BF)

    def copy(k, out_ref):
        return pltpu.make_async_copy(packed.at[k], out_ref.at[owner_ref[k]], sems.at[k])

    for k in range(regions):
        padded[k % 4, :, 0:RES, :] = grad_ref[k]
        packed[k] = dot(perm, padded[k % 4].reshape(FLAT, CH)).astype(BF)
        for s, out_ref in enumerate((out_zero, out_one)):
            pl.when(slot_ref[k] == s)(copy(k, out_ref).start)
    for k in range(regions):
        copy(k, out_zero).wait()


def pack_upstream(plan, upstream, owners):
    regions = upstream.shape[0]
    return pl.pallas_call(
        pack_kernel,
        grid_spec=pltpu.PrefetchScalarGridSpec(
            num_scalar_prefetch=2,
            grid=(1,),
            in_specs=[pl.BlockSpec(upstream.shape, lambda i, *_: (0, 0, 0, 0))],
            out_specs=[pl.BlockSpec(memory_space=pl.ANY)] * 2,
            scratch_shapes=[
                pltpu.VMEM((4, RES, PITCH, CH), BF),
                pltpu.VMEM((regions, PACK, CH), BF),
                pltpu.SemaphoreType.DMA((regions,)),
            ],
        ),
        out_shape=[jax.ShapeDtypeStruct((owners, PACK, CH), BF)] * 2,
        compiler_params=pltpu.CompilerParams(vmem_limit_bytes=VMEM),
    )(*plan, upstream)


def put_shifted(ref, r, value):
    ref[r, PITCH : PITCH + FLAT, 0:CH] = pltpu.roll(value, 1, 0).astype(BF)
    ref[r, PITCH : PITCH + FLAT, CH : 2 * CH] = value.astype(BF)
    ref[r, PITCH : PITCH + FLAT, 2 * CH : WIDE] = pltpu.roll(value, FLAT - 1, 0).astype(BF)


def clear_edges(ref):
    edge = jnp.zeros((ref.shape[0], PITCH, WIDE), BF)
    ref[:, 0:PITCH, :] = edge
    ref[:, PITCH + FLAT : 2 * PITCH + FLAT, :] = edge


def conv(ref, r, kernel_ref, a):
    return dot(ref[r, PITCH * a : PITCH * a + FLAT, :], kernel_ref[3 * a : 3 * a + 3].reshape(WIDE, CH))


def conv_back(ref, r, kernel_ref):
    sides = [ref[r, PITCH * a : PITCH * a + FLAT, :] for a in range(3)]
    return dot(jnp.concatenate(sides, axis=1), kernel_ref[...].reshape(9 * CH, CH))


def sampled_block(geo_ref, slot, tile_ref):
    row0, row_step = geo_ref[slot * 4], geo_ref[slot * 4 + 1]
    col0, col_step = geo_ref[slot * 4 + 2], geo_ref[slot * 4 + 3]
    lane, sub = iota((PITCH, CH), 1), iota((PITCH, CH), 0)
    reach = 16 - jnp.abs(16 * (lane & 31) - (col0 + col_step * sub))
    col_weight = jnp.where(sub < RES, jnp.maximum(reach, 0), 0).astype(F32)
    lower = (lane & 32) == 0
    owner = lane >> 6
    pieces = []
    for first in range(0, RES, 4):
        members = range(first, min(first + 4, RES))
        weights, rows = [], []
        for p in members:
            place = row0 + row_step * p
            low = place >> 4
            share = (place & 15).astype(F32) * (1.0 / 256.0)
            row_weight = jnp.where(lower, 1.0 / 16.0 - share, share)
            weights.append(jnp.where(owner == p - first, row_weight * col_weight, 0.0).astype(BF))
            rows.append(tile_ref[pl.ds(low, 2)].reshape(2 * TW, CH))
        depth = 64 * len(rows)
        left = jnp.concatenate(weights, axis=0)[:, 0:depth]
        pieces.append(dot(left, jnp.concatenate(rows, axis=0)))
    return jnp.concatenate(pieces, axis=0)


def sigmoid(v):
    return 0.5 * jnp.tanh(0.5 * v) + 0.5


def forward_kernel(steps_ref, list_ref, live_ref, geo_ref, *refs):
    first_ref, second_ref, _, turned_ref, wide_in, wide_hid = refs[1:]
    step = pl.program_id(0)

    @pl.when(step == 0)
    def _():
        clear_edges(wide_in)
        clear_edges(wide_hid)
        for w, kernel_ref in enumerate((first_ref, second_ref)):
            for n in range(9):
                turned_ref[w, n] = kernel_ref[8 - n].T

    full = live_ref[step * PER + PER // 2] > 0
    for per, chosen in ((PER, full), (PER // 2, jnp.logical_not(full))):
        run = functools.partial(forward_step, per, list_ref, geo_ref, *refs)
        pl.when((step < steps_ref[0]) & chosen)(run)


def forward_step(per, list_ref, geo_ref, tile_ref, first_ref, second_ref, out_ref, turned_ref, wide_in, wide_hid):
    step = pl.program_id(0)
    inside = (iota((FLAT, CH), 0) & 15) < RES

    def sample(r):
        block = sampled_block(geo_ref, list_ref[step * PER + r], tile_ref)
        put_shifted(wide_in, r, block)
        out_ref[r, 0] = block.astype(BF)

    def hide(r, pre):
        gate = sigmoid(pre)
        hidden = jnp.where(inside, pre * gate, 0.0)
        put_shifted(wide_hid, r, hidden)
        out_ref[r, 1] = hidden.astype(BF)
        out_ref[r, 2] = jnp.where(inside, gate + hidden * (1.0 - gate), 0.0).astype(BF)

    def finish(r, pre):
        gate = sigmoid(pre)
        out_ref[r, 3] = (gate * (1.0 + pre * (1.0 - gate))).astype(BF)

    sample(0)
    held_pre = None
    for r in range(per):
        pre = conv(wide_in, r, first_ref, 0)
        if r + 1 < per:
            sample(r + 1)
        pre += conv(wide_in, r, first_ref, 1)
        if r:
            hide(r - 1, held_pre)
        pre += conv(wide_in, r, first_ref, 2)
        held_pre = pre
    last = held_pre
    for r in range(per):
        pre = conv(wide_hid, r, second_ref, 0)
        if r == 0:
            hide(per - 1, last)
        else:
            finish(r - 1, held_pre)
        pre += conv(wide_hid, r, second_ref, 1)
        pre += conv(wide_hid, r, second_ref, 2)
        held_pre = pre
    finish(per - 1, held_pre)


PER = 4


def held(step, steps_ref):
    return jnp.minimum(step, steps_ref[0] - 1)


def forward(steps, slots, live, geo, tile, first, second):
    count = slots.shape[0]
    whole = lambda *shape: pl.BlockSpec(shape, lambda i, *_: (0,) * len(shape))
    return pl.pallas_call(
        forward_kernel,
        grid_spec=pltpu.PrefetchScalarGridSpec(
            num_scalar_prefetch=4,
            grid=(count // PER,),
            in_specs=[whole(TH, TW, CH), whole(9, CH, CH), whole(9, CH, CH)],
            out_specs=[
                pl.BlockSpec((PER, 4, FLAT, CH), lambda i, n, *_: (held(i, n), 0, 0, 0)),
                whole(2, 9, CH, CH),
            ],
            scratch_shapes=[
                pltpu.VMEM((PER, FLAT + 2 * PITCH, WIDE), BF),
                pltpu.VMEM((PER, FLAT + 2 * PITCH, WIDE), BF),
            ],
        ),
        out_shape=[
            jax.ShapeDtypeStruct((count, 4, FLAT, CH), BF),
            jax.ShapeDtypeStruct((2, 9, CH, CH), BF),
        ],
        compiler_params=pltpu.CompilerParams(vmem_limit_bytes=VMEM),
    )(steps, slots, live, geo, tile, first, second)


def spread(geo_ref, slot, back, grad_ref, half):
    up, along = iota((CH, 128), 0), iota((CH, 128), 1)
    col0, col_step = geo_ref[slot * 4 + 2], geo_ref[slot * 4 + 3]
    same = ((along & 15) < RES) & ((up >> 5) == (along >> 4))
    reach = 16 - jnp.abs(16 * (up & 31) - (col0 + col_step * (along & 15)))
    weight = jnp.where(same, jnp.maximum(reach, 0), 0).astype(F32) * (1.0 / 16.0)
    first = 8 * half
    members = min(8, RES - first)
    stripes = dot(
        weight[0 : members * TW, 0 : members * PITCH].astype(BF),
        back[first * PITCH : (first + members) * PITCH],
    )
    for k in range(members):
        place = geo_ref[slot * 4] + geo_ref[slot * 4 + 1] * (first + k)
        low = place >> 4
        share = (place & 15).astype(F32) * (1.0 / 16.0)
        stripe = stripes[k * TW : (k + 1) * TW]
        upper = share * stripe
        pair = jnp.concatenate([(stripe - upper)[None], upper[None]], axis=0)
        grad_ref[pl.ds(low, 2)] = grad_ref[pl.ds(low, 2)] + pair


def backward_step(per, at, list_ref, live_ref, geo_ref, kept_ref, ups, first_ref, second_ref, scratch):
    wide_two, wide_one, first_acc, second_acc, tile_acc = scratch
    unpack = (iota((FLAT, PACK), 1) == packed_place(iota((FLAT, PACK), 0))).astype(F32).astype(BF)
    def upstream(r):
        packed = jnp.where(live_ref[at + r] > 0, ups[r][0], jnp.zeros_like(ups[r][0]))
        put_shifted(wide_two, r, dot(unpack, packed) * kept_ref[r, 3].astype(F32))

    def first_delta(r, hidden_back):
        put_shifted(wide_one, r, hidden_back * kept_ref[r, 2].astype(F32))

    def give_back(r, back, half):
        spread(geo_ref, list_ref[at + r], back, tile_acc, half)

    upstream(0)
    upstream(1)
    held = []
    for r in range(per):
        held.append(conv_back(wide_two, r, second_ref))
        if r + 2 < per:
            upstream(r + 2)
        if r:
            first_delta(r - 1, held[r - 1])
    kernel_sums(per, kept_ref, 1, wide_two, second_acc, 0)
    first_delta(per - 1, held[per - 1])
    kernel_sums(per, kept_ref, 1, wide_two, second_acc, 1)
    kernel_sums(per, kept_ref, 1, wide_two, second_acc, 2)
    held = []
    for r in range(per):
        held.append(conv_back(wide_one, r, first_ref).astype(BF))
    for a in range(3):
        kernel_sums(per, kept_ref, 0, wide_one, first_acc, a)
        if a < per:
            give_back(a, held[a], 0)
            give_back(a, held[a], 1)
    for r in range(3, per):
        give_back(r, held[r], 0)
        give_back(r, held[r], 1)


def kernel_sums(per, kept_ref, which, wide, acc, a):
    values = kept_ref[0:per, which].reshape(per * FLAT, CH)
    acc[a] += lax.dot_general(
        values, wide[0:per, PITCH * a : PITCH * a + FLAT, :].reshape(per * FLAT, WIDE),
        (((0,), (0,)), ((), ())), preferred_element_type=F32,
    )


def backward_kernel(begun, scale, steps_ref, list_ref, live_ref, geo_ref, kept_ref, *refs):
    ups, refs = refs[:PER], refs[PER:]
    turned_ref, refs = refs[0], refs[1:]
    if begun:
        sums, (tile_out, kernels_out), refs = refs[:3], refs[3:5], refs[5:]
        scratch, fetched, sems = refs[:5], refs[5:8], refs[8]
        fetches = [pltpu.make_async_copy(a, b, sems.at[n]) for n, (a, b) in enumerate(zip(sums, fetched))]
    else:
        scratch, fetches = refs[3:5] + refs[:3], []
    wide_two, wide_one, first_acc, second_acc, tile_acc = scratch
    first_ref, second_ref = turned_ref.at[0], turned_ref.at[1]
    step = pl.program_id(0)

    @pl.when(step == 0)
    def _():
        for fetch in fetches:
            fetch.start()
        clear_edges(wide_two)
        clear_edges(wide_one)
        first_acc[...] = jnp.zeros_like(first_acc)
        second_acc[...] = jnp.zeros_like(second_acc)
        tile_acc[...] = jnp.zeros_like(tile_acc)

    at = (steps_ref[1] + step) * PER
    within = step < steps_ref[0]
    full = live_ref[jnp.minimum(at + PER // 2, live_ref.shape[0] - 1)] > 0
    for per, chosen in ((PER, full), (PER // 2, jnp.logical_not(full))):
        run = functools.partial(
            backward_step, per, at, list_ref, live_ref, geo_ref, kept_ref, ups, first_ref, second_ref, scratch
        )
        pl.when(within & chosen)(run)

    if begun:

        @pl.when(step == pl.num_programs(0) - 1)
        def _():
            for fetch in fetches:
                fetch.wait()
            tile_out[...] = (tile_acc[...] + fetched[2][...]).astype(BF)
            for n in range(9):
                row, cols = (8 - n) // 3, slice((8 - n) % 3 * CH, ((8 - n) % 3 + 1) * CH)
                for w, acc in enumerate((first_acc, second_acc)):
                    total = acc[row, :, cols] + fetched[w][row, :, cols]
                    kernels_out[w, n * CH : (n + 1) * CH] = (total * scale).astype(BF)


def backward(slot, plan, geo, kept, arrived, turned, sums, scale):
    steps, slots, live = plan
    readers = arrived.shape[0]
    begun = sums is not None
    whole = lambda *shape: pl.BlockSpec(shape, lambda i, *_: (0,) * len(shape))
    last = slots.shape[0] // PER - 1

    def group(i, n):
        return jnp.clip(n[1] + jnp.minimum(i, n[0] - 1), 0, last)

    def from_reader(j):
        def block(i, n, s, *_):
            return jnp.clip(s[PER * group(i, n) + j] - slot * readers, 0, readers - 1), 0, 0

        return pl.BlockSpec((1, PACK, CH), block)

    totals = [(3, CH, WIDE), (3, CH, WIDE), (TH, TW, CH)]
    wide = [pltpu.VMEM((PER, FLAT + 2 * PITCH, WIDE), BF)] * 2
    if begun:
        outs = [jax.ShapeDtypeStruct((TH, TW, CH), BF), jax.ShapeDtypeStruct((2, 9 * CH, CH), BF)]
        scratch = wide + [pltpu.VMEM(t, F32) for t in totals] * 2 + [pltpu.SemaphoreType.DMA((3,))]
    else:
        outs = [jax.ShapeDtypeStruct(t, F32) for t in totals]
        scratch = wide
    return pl.pallas_call(
        functools.partial(backward_kernel, begun, scale),
        grid_spec=pltpu.PrefetchScalarGridSpec(
            num_scalar_prefetch=4,
            grid=(readers // PER,),
            in_specs=[
                pl.BlockSpec((PER, 4, FLAT, CH), lambda i, n, *_: (group(i, n), 0, 0, 0)),
                *[from_reader(j) for j in range(PER)],
                whole(2, 9, CH, CH),
                *[pl.BlockSpec(memory_space=pl.ANY)] * (3 if begun else 0),
            ],
            out_specs=[whole(*o.shape) for o in outs],
            scratch_shapes=scratch,
        ),
        out_shape=outs,
        compiler_params=pltpu.CompilerParams(vmem_limit_bytes=VMEM),
    )(steps, slots, live, geo, kept, *[arrived] * PER, turned, *(sums or ()))


SIDE = 4
ORDERS = ((0, 1, 2), (1, 2, 0), (2, 0, 1))


def reduce_kernel(mine_ref, out_ref, pair_in, half, in_one, held_one, in_two, held_two, in_three, sems_s, sems_r):
    tile, line = lax.axis_index("tile"), lax.axis_index("group")
    core, x, z = tile & 1, (tile >> 1) & 3, tile >> 3
    coords = (z, x, line)
    third = mine_ref.shape[1] // 3
    quarter, small = third // SIDE, third // SIDE // SIDE

    def peer(axis, k):
        to = (coords[axis] + k) & (SIDE - 1)
        if axis == 0:
            return {"tile": to * 8 + x * 2 + core}
        if axis == 1:
            return {"tile": z * 8 + to * 2 + core}
        return {"group": to}

    other = {"tile": tile + 1 - 2 * core}

    def rows(start, size):
        return pl.ds(pl.multiple_of(start, 16), size)

    def remote(source, target, sem, device):
        return pltpu.make_async_remote_copy(
            source, target, sems_s.at[sem], sems_r.at[sem], device_id=device, device_id_type=MESH
        )

    barrier = pltpu.get_barrier_semaphore()
    pl.semaphore_signal(barrier, inc=1, device_id=other, device_id_type=MESH)
    for axis in range(3):
        for k in range(1, SIDE):
            pl.semaphore_signal(barrier, inc=1, device_id=peer(axis, k), device_id_type=MESH)
    pl.semaphore_wait(barrier, 1 + 3 * (SIDE - 1))

    def sem(stage, part, k):
        return 6 + (stage * 3 + part) * 3 + k - 1

    def swap(part):
        at = slice(part * third, (part + 1) * third)
        return remote(mine_ref.at[1 - core, at], pair_in.at[at], part, other)

    def one(part, k):
        axis = ORDERS[part][0]
        to = (coords[axis] + k) & (SIDE - 1)
        source = half.at[rows(part * third + to * quarter, quarter)]
        return remote(source, in_one.at[part, k - 1], sem(0, part, k), peer(axis, k))

    def two(part, k):
        axis = ORDERS[part][1]
        to = (coords[axis] + k) & (SIDE - 1)
        source = held_one.at[part, rows(to * small, small)]
        return remote(source, in_two.at[part, k - 1], sem(1, part, k), peer(axis, k))

    def three(part, k):
        return remote(held_two.at[part], in_three.at[part, k - 1], sem(2, part, k), peer(ORDERS[part][2], k))

    def start_of(part, first, second):
        return part * third + first * quarter + second * small

    def back_two(part, k, sender):
        first, second = ORDERS[part][:2]
        at = rows(start_of(part, coords[first], sender), small)
        return remote(out_ref.at[core, at], out_ref.at[core, at], sem(3, part, k), peer(second, k))

    def back_one(part, k, sender):
        first = ORDERS[part][0]
        at = rows(part * third + sender * quarter, quarter)
        return remote(out_ref.at[core, at], out_ref.at[core, at], sem(4, part, k), peer(first, k))

    def give(part, of):
        at = slice(part * third, (part + 1) * third)
        return remote(out_ref.at[of, at], out_ref.at[of, at], 3 + part, other)

    shifts = range(1, SIDE)
    parts = range(3)
    for part in parts:
        swap(part).start()
    for part in parts:
        swap(part).wait()
        at = slice(part * third, (part + 1) * third)
        half[at] = (mine_ref[core, at].astype(F32) + pair_in[at].astype(F32)).astype(BF)
        for k in shifts:
            one(part, k).start()
    for part in parts:
        own = coords[ORDERS[part][0]]
        total = half[rows(part * third + own * quarter, quarter)].astype(F32)
        for k in shifts:
            one(part, k).wait()
            total += in_one[part, k - 1].astype(F32)
        held_one[part] = total.astype(BF)
        for k in shifts:
            two(part, k).start()
    for part in parts:
        own = coords[ORDERS[part][1]]
        total = held_one[part, rows(own * small, small)].astype(F32)
        for k in shifts:
            two(part, k).wait()
            total += in_two[part, k - 1].astype(F32)
        held_two[part] = total.astype(BF)
        for k in shifts:
            three(part, k).start()
    for part in parts:
        first, second, axis = ORDERS[part]
        terms = [held_two[part].astype(F32)]
        for k in shifts:
            three(part, k).wait()
            terms.append(in_three[part, k - 1].astype(F32))
        total = None
        for place in range(SIDE):
            back = (coords[axis] - place) & (SIDE - 1)
            term = terms[0]
            for k in shifts:
                term = jnp.where(back == k, terms[k], term)
            total = term if total is None else total + term
        out_ref[core, rows(start_of(part, coords[first], coords[second]), small)] = total.astype(BF)
        for k in shifts:
            back_two(part, k, coords[second]).start()
    for part in parts:
        first, second, axis = ORDERS[part]
        for k in shifts:
            back_two(part, k, coords[second]).wait_send()
            back_two(part, k, (coords[second] - k) & (SIDE - 1)).wait_recv()
        for k in shifts:
            back_one(part, k, coords[first]).start()
    for part in parts:
        first = ORDERS[part][0]
        for k in shifts:
            back_one(part, k, coords[first]).wait_send()
            back_one(part, k, (coords[first] - k) & (SIDE - 1)).wait_recv()
        give(part, core).start()
    for part in parts:
        give(part, core).wait_send()
        give(part, 1 - core).wait_recv()


def reduce_everywhere(mine):
    rows = mine.shape[1]
    third = rows // 3
    quarter, small = third // SIDE, third // SIDE // SIDE
    spec = pl.BlockSpec(memory_space=pltpu.VMEM)
    return pl.pallas_call(
        reduce_kernel,
        in_specs=[spec],
        out_specs=spec,
        out_shape=jax.ShapeDtypeStruct(mine.shape, BF),
        scratch_shapes=[
            pltpu.VMEM((rows, CH), BF),
            pltpu.VMEM((rows, CH), BF),
            pltpu.VMEM((3, SIDE - 1, quarter, CH), BF),
            pltpu.VMEM((3, quarter, CH), BF),
            pltpu.VMEM((3, SIDE - 1, small, CH), BF),
            pltpu.VMEM((3, small, CH), BF),
            pltpu.VMEM((3, SIDE - 1, small, CH), BF),
            pltpu.SemaphoreType.DMA((6 + 45,)),
            pltpu.SemaphoreType.DMA((6 + 45,)),
        ],
        compiler_params=pltpu.CompilerParams(
            collective_id=0, has_side_effects=True, vmem_limit_bytes=VMEM
        ),
    )(mine)


def send_plan(column, regions):
    owners = column.shape[0]
    ids = jnp.arange(owners, dtype=jnp.int32)
    before = jnp.sum(jnp.where(ids[None, :] < ids[:, None], column[None, :], 0), axis=1)
    k = jnp.arange(regions, dtype=jnp.int32)[:, None]
    mine = (before[None, :] <= k) & (k < (before + column)[None, :])
    slot = jnp.sum(jnp.where(mine, k - before[None, :], 0), axis=1, dtype=jnp.int32)
    owner = jnp.sum(jnp.where(mine, ids[None, :], 0), axis=1, dtype=jnp.int32)
    return slot, owner


def work_plan(row):
    readers = row.shape[0]
    ids = jnp.arange(readers, dtype=jnp.int32)
    place = jnp.arange(2 * readers, dtype=jnp.int32)[:, None]
    steps_zero = (jnp.sum(row > 0, dtype=jnp.int32) + PER - 1) // PER
    steps_one = (jnp.sum(row > 1, dtype=jnp.int32) + PER - 1) // PER
    slots, live = 0, 0
    for s, start in ((0, 0), (1, PER * steps_zero)):
        has = row > s
        rank = jnp.sum(jnp.where((ids[None, :] < ids[:, None]) & has[None, :], 1, 0), axis=1)
        hit = has[None, :] & (start + rank[None, :] == place)
        slots += jnp.sum(jnp.where(hit, s * readers + ids[None, :], 0), axis=1, dtype=jnp.int32)
        live += jnp.sum(hit, axis=1, dtype=jnp.int32)
    zero = jnp.stack([steps_zero, jnp.zeros_like(steps_zero)])
    one = jnp.stack([steps_one, steps_zero])
    return slots, live, jnp.maximum(steps_zero + steps_one, 1).reshape(1), zero, one


def exchange(blocks):
    return lax.all_to_all(blocks, "tile", split_axis=0, concat_axis=0, tiled=True)


def on_device(features, out_grad, pair_count, sample_grid, first_kernel, second_kernel):
    tiles, lines = lax.axis_size("tile"), lax.axis_size("group")
    own = lax.axis_index("tile")
    counts = pair_count[0]
    upstream = out_grad[0]
    regions = upstream.shape[0]
    column = lax.dynamic_index_in_dim(counts, own, 1, keepdims=False)
    row = lax.dynamic_index_in_dim(counts, own, 0, keepdims=False)

    packed = pack_upstream(send_plan(column, regions), upstream, tiles)
    arrived = [exchange(packed[0])]

    grid = jnp.swapaxes(sample_grid[0, 0], 0, 1).reshape(2 * tiles, 4, RES)
    row_at = 16 * grid[:, 0, 0:2] + grid[:, 1, 0:2]
    col_at = 16 * grid[:, 2, 0:2] + grid[:, 3, 0:2]
    geo = jnp.stack(
        [row_at[:, 0], row_at[:, 1] - row_at[:, 0], col_at[:, 0], col_at[:, 1] - col_at[:, 0]],
        axis=1,
    ).reshape(-1)
    slots, live, steps, zero, one = work_plan(row)
    first, second = first_kernel.reshape(9, CH, CH), second_kernel.reshape(9, CH, CH)
    kept, turned = forward(steps, slots, live, geo, features[0], first, second)
    later, kept = lax.optimization_barrier((packed[1], kept))
    arrived.append(exchange(later))
    scale = 1.0 / math.sqrt(lines * tiles * regions * RES * RES)
    sums = backward(0, (zero, slots, live), geo, kept, arrived[0], turned, None, scale)
    tile_grad, parts = backward(1, (one, slots, live), geo, kept, arrived[1], turned, sums, scale)
    totals = reduce_everywhere(parts).astype(F32).reshape(2, 3, 3, CH, CH)
    return tile_grad[None], totals[0], totals[1]


def solution(mesh):
    return jax.shard_map(
        on_device,
        mesh=mesh,
        in_specs=(
            P("group", "tile", None, None),
            P("group", "tile", None, None, None),
            P("group", None, None),
            P("group", "tile", None, None, None, None),
            P(),
            P(),
        ),
        out_specs=(P("group", "tile", None, None), P(), P()),
        check_vma=False,
    )
```

```python
import functools
import math

import jax
import jax.numpy as jnp
from jax import lax
from jax.experimental import pallas as pl
from jax.experimental.pallas import tpu as pltpu
from jax.sharding import PartitionSpec as P

BF = jnp.bfloat16
F32 = jnp.float32
MESH = pl.DeviceIdType.MESH
RES = 14
PITCH = 16
FLAT = RES * PITCH
PACK = 200
CH = 256
WIDE = 3 * CH
TH = 64
TW = 32
VMEM = 60 * 1024 * 1024


def iota(shape, dim):
    return lax.broadcasted_iota(jnp.int32, shape, dim)


def dot(a, b):
    return jnp.dot(a, b, preferred_element_type=F32)


def packed_place(col):
    return jnp.where((col & 15) < RES, (col >> 4) * RES + (col & 15), -1)


def pack_kernel(slot_ref, owner_ref, grad_ref, out_zero, out_one, padded, packed, sems):
    regions = grad_ref.shape[0]
    padded[...] = jnp.zeros_like(padded)
    perm = (iota((PACK, FLAT), 0) == packed_place(iota((PACK, FLAT), 1))).astype(F32).astype(BF)

    def copy(k, out_ref):
        return pltpu.make_async_copy(packed.at[k], out_ref.at[owner_ref[k]], sems.at[k])

    for k in range(regions):
        padded[k % 4, :, 0:RES, :] = grad_ref[k]
        packed[k] = dot(perm, padded[k % 4].reshape(FLAT, CH)).astype(BF)
        for s, out_ref in enumerate((out_zero, out_one)):
            pl.when(slot_ref[k] == s)(copy(k, out_ref).start)
    for k in range(regions):
        copy(k, out_zero).wait()


def pack_upstream(plan, upstream, owners):
    regions = upstream.shape[0]
    return pl.pallas_call(
        pack_kernel,
        grid_spec=pltpu.PrefetchScalarGridSpec(
            num_scalar_prefetch=2,
            grid=(1,),
            in_specs=[pl.BlockSpec(upstream.shape, lambda i, *_: (0, 0, 0, 0))],
            out_specs=[pl.BlockSpec(memory_space=pl.ANY)] * 2,
            scratch_shapes=[
                pltpu.VMEM((4, RES, PITCH, CH), BF),
                pltpu.VMEM((regions, PACK, CH), BF),
                pltpu.SemaphoreType.DMA((regions,)),
            ],
        ),
        out_shape=[jax.ShapeDtypeStruct((owners, PACK, CH), BF)] * 2,
        compiler_params=pltpu.CompilerParams(vmem_limit_bytes=VMEM),
    )(*plan, upstream)


def put_shifted(ref, r, value):
    ref[r, PITCH : PITCH + FLAT, 0:CH] = pltpu.roll(value, 1, 0).astype(BF)
    ref[r, PITCH : PITCH + FLAT, CH : 2 * CH] = value.astype(BF)
    ref[r, PITCH : PITCH + FLAT, 2 * CH : WIDE] = pltpu.roll(value, FLAT - 1, 0).astype(BF)


def clear_edges(ref):
    edge = jnp.zeros((ref.shape[0], PITCH, WIDE), BF)
    ref[:, 0:PITCH, :] = edge
    ref[:, PITCH + FLAT : 2 * PITCH + FLAT, :] = edge


def conv(ref, r, kernel_ref, a):
    return dot(ref[r, PITCH * a : PITCH * a + FLAT, :], kernel_ref[3 * a : 3 * a + 3].reshape(WIDE, CH))


def conv_back(ref, r, kernel_ref):
    sides = [ref[r, PITCH * a : PITCH * a + FLAT, :] for a in range(3)]
    return dot(jnp.concatenate(sides, axis=1), kernel_ref[...].reshape(9 * CH, CH))


def sampled_block(geo_ref, slot, tile_ref):
    row0, row_step = geo_ref[slot * 4], geo_ref[slot * 4 + 1]
    col0, col_step = geo_ref[slot * 4 + 2], geo_ref[slot * 4 + 3]
    lane, sub = iota((PITCH, CH), 1), iota((PITCH, CH), 0)
    reach = 16 - jnp.abs(16 * (lane & 31) - (col0 + col_step * sub))
    col_weight = jnp.where(sub < RES, jnp.maximum(reach, 0), 0).astype(F32)
    lower = (lane & 32) == 0
    owner = lane >> 6
    pieces = []
    for first in range(0, RES, 4):
        members = range(first, min(first + 4, RES))
        weights, rows = [], []
        for p in members:
            place = row0 + row_step * p
            low = place >> 4
            share = (place & 15).astype(F32) * (1.0 / 256.0)
            row_weight = jnp.where(lower, 1.0 / 16.0 - share, share)
            weights.append(jnp.where(owner == p - first, row_weight * col_weight, 0.0).astype(BF))
            rows.append(tile_ref[pl.ds(low, 2)].reshape(2 * TW, CH))
        depth = 64 * len(rows)
        left = jnp.concatenate(weights, axis=0)[:, 0:depth]
        pieces.append(dot(left, jnp.concatenate(rows, axis=0)))
    return jnp.concatenate(pieces, axis=0)


def sigmoid(v):
    return 0.5 * jnp.tanh(0.5 * v) + 0.5


def forward_kernel(steps_ref, list_ref, live_ref, geo_ref, *refs):
    first_ref, second_ref, _, turned_ref, wide_in, wide_hid = refs[1:]
    step = pl.program_id(0)

    @pl.when(step == 0)
    def _():
        clear_edges(wide_in)
        clear_edges(wide_hid)
        for w, kernel_ref in enumerate((first_ref, second_ref)):
            for n in range(9):
                turned_ref[w, n] = kernel_ref[8 - n].T

    full = live_ref[step * PER + PER // 2] > 0
    for per, chosen in ((PER, full), (PER // 2, jnp.logical_not(full))):
        run = functools.partial(forward_step, per, list_ref, geo_ref, *refs)
        pl.when((step < steps_ref[0]) & chosen)(run)


def forward_step(per, list_ref, geo_ref, tile_ref, first_ref, second_ref, out_ref, turned_ref, wide_in, wide_hid):
    step = pl.program_id(0)
    inside = (iota((FLAT, CH), 0) & 15) < RES

    def sample(r):
        block = sampled_block(geo_ref, slot_at(list_ref, step * PER + r), tile_ref)
        put_shifted(wide_in, r, block)
        out_ref[r, 0] = block.astype(BF)

    def hide(r, pre):
        gate = sigmoid(pre)
        hidden = jnp.where(inside, pre * gate, 0.0)
        put_shifted(wide_hid, r, hidden)
        out_ref[r, 1] = hidden.astype(BF)
        out_ref[r, 2] = jnp.where(inside, gate + hidden * (1.0 - gate), 0.0).astype(BF)

    def finish(r, pre):
        gate = sigmoid(pre)
        out_ref[r, 3] = (gate * (1.0 + pre * (1.0 - gate))).astype(BF)

    sample(0)
    held_pre = None
    for r in range(per):
        pre = conv(wide_in, r, first_ref, 0)
        if r + 1 < per:
            sample(r + 1)
        pre += conv(wide_in, r, first_ref, 1)
        if r:
            hide(r - 1, held_pre)
        pre += conv(wide_in, r, first_ref, 2)
        held_pre = pre
    last = held_pre
    for r in range(per):
        pre = conv(wide_hid, r, second_ref, 0)
        if r == 0:
            hide(per - 1, last)
        else:
            finish(r - 1, held_pre)
        pre += conv(wide_hid, r, second_ref, 1)
        pre += conv(wide_hid, r, second_ref, 2)
        held_pre = pre
    finish(per - 1, held_pre)


PER = 4


def slot_at(list_ref, place):
    return jnp.maximum(list_ref[place] - 1, 0)


def held(step, steps_ref):
    return jnp.minimum(step, steps_ref[0] - 1)


def forward(steps, slots, live, geo, tile, first, second):
    count = slots.shape[0]
    whole = lambda *shape: pl.BlockSpec(shape, lambda i, *_: (0,) * len(shape))
    return pl.pallas_call(
        forward_kernel,
        grid_spec=pltpu.PrefetchScalarGridSpec(
            num_scalar_prefetch=4,
            grid=(count // PER,),
            in_specs=[whole(TH, TW, CH), whole(9, CH, CH), whole(9, CH, CH)],
            out_specs=[
                pl.BlockSpec((PER, 4, FLAT, CH), lambda i, n, *_: (held(i, n), 0, 0, 0)),
                whole(2, 9, CH, CH),
            ],
            scratch_shapes=[
                pltpu.VMEM((PER, FLAT + 2 * PITCH, WIDE), BF),
                pltpu.VMEM((PER, FLAT + 2 * PITCH, WIDE), BF),
            ],
        ),
        out_shape=[
            jax.ShapeDtypeStruct((count, 4, FLAT, CH), BF),
            jax.ShapeDtypeStruct((2, 9, CH, CH), BF),
        ],
        compiler_params=pltpu.CompilerParams(vmem_limit_bytes=VMEM),
    )(steps, slots, live, geo, tile, first, second)


def spread(geo_ref, slot, back, grad_ref, half):
    up, along = iota((CH, 128), 0), iota((CH, 128), 1)
    col0, col_step = geo_ref[slot * 4 + 2], geo_ref[slot * 4 + 3]
    same = ((along & 15) < RES) & ((up >> 5) == (along >> 4))
    reach = 16 - jnp.abs(16 * (up & 31) - (col0 + col_step * (along & 15)))
    weight = jnp.where(same, jnp.maximum(reach, 0), 0).astype(F32) * (1.0 / 16.0)
    first = 8 * half
    members = min(8, RES - first)
    stripes = dot(
        weight[0 : members * TW, 0 : members * PITCH].astype(BF),
        back[first * PITCH : (first + members) * PITCH],
    )
    for k in range(members):
        place = geo_ref[slot * 4] + geo_ref[slot * 4 + 1] * (first + k)
        low = place >> 4
        share = (place & 15).astype(F32) * (1.0 / 16.0)
        stripe = stripes[k * TW : (k + 1) * TW]
        upper = share * stripe
        pair = jnp.concatenate([(stripe - upper)[None], upper[None]], axis=0)
        grad_ref[pl.ds(low, 2)] = grad_ref[pl.ds(low, 2)] + pair


def backward_step(per, at, list_ref, live_ref, geo_ref, kept_ref, ups, first_ref, second_ref, scratch):
    wide_two, wide_one, first_acc, second_acc, tile_acc = scratch
    unpack = (iota((FLAT, PACK), 1) == packed_place(iota((FLAT, PACK), 0))).astype(F32).astype(BF)
    def upstream(r):
        packed = jnp.where(live_ref[at + r] > 0, ups[r][0], jnp.zeros_like(ups[r][0]))
        put_shifted(wide_two, r, dot(unpack, packed) * kept_ref[r, 3].astype(F32))

    def first_delta(r, hidden_back):
        put_shifted(wide_one, r, hidden_back * kept_ref[r, 2].astype(F32))

    def give_back(r, back, half):
        spread(geo_ref, slot_at(list_ref, at + r), back, tile_acc, half)

    upstream(0)
    upstream(1)
    held = []
    for r in range(per):
        held.append(conv_back(wide_two, r, second_ref))
        if r + 2 < per:
            upstream(r + 2)
        if r:
            first_delta(r - 1, held[r - 1])
    kernel_sums(per, kept_ref, 1, wide_two, second_acc, 0)
    first_delta(per - 1, held[per - 1])
    kernel_sums(per, kept_ref, 1, wide_two, second_acc, 1)
    kernel_sums(per, kept_ref, 1, wide_two, second_acc, 2)
    held = []
    for r in range(per):
        held.append(conv_back(wide_one, r, first_ref).astype(BF))
    for a in range(3):
        kernel_sums(per, kept_ref, 0, wide_one, first_acc, a)
        if a < per:
            give_back(a, held[a], 0)
            give_back(a, held[a], 1)
    for r in range(3, per):
        give_back(r, held[r], 0)
        give_back(r, held[r], 1)


def kernel_sums(per, kept_ref, which, wide, acc, a):
    values = kept_ref[0:per, which].reshape(per * FLAT, CH)
    acc[a] += lax.dot_general(
        values, wide[0:per, PITCH * a : PITCH * a + FLAT, :].reshape(per * FLAT, WIDE),
        (((0,), (0,)), ((), ())), preferred_element_type=F32,
    )


def base(slot, steps_ref):
    return steps_ref[1] if slot else 0


def backward_kernel(slot, begun, scale, steps_ref, list_ref, live_ref, geo_ref, kept_ref, *refs):
    ups, refs = refs[:PER], refs[PER:]
    turned_ref, refs = refs[0], refs[1:]
    if begun:
        sums, (tile_out, kernels_out), refs = refs[:3], refs[3:5], refs[5:]
        scratch, fetched, sems = refs[:5], refs[5:8], refs[8]
        fetches = [pltpu.make_async_copy(a, b, sems.at[n]) for n, (a, b) in enumerate(zip(sums, fetched))]
    else:
        scratch, fetches = refs[3:5] + refs[:3], []
    wide_two, wide_one, first_acc, second_acc, tile_acc = scratch
    first_ref, second_ref = turned_ref.at[0], turned_ref.at[1]
    step = pl.program_id(0)

    @pl.when(step == 0)
    def _():
        for fetch in fetches:
            fetch.start()
        clear_edges(wide_two)
        clear_edges(wide_one)
        first_acc[...] = jnp.zeros_like(first_acc)
        second_acc[...] = jnp.zeros_like(second_acc)
        tile_acc[...] = jnp.zeros_like(tile_acc)

    at = (base(slot, steps_ref) + step) * PER
    within = step < steps_ref[1 + slot]
    full = live_ref[jnp.minimum(at + PER // 2, live_ref.shape[0] - 1)] > 0
    for per, chosen in ((PER, full), (PER // 2, jnp.logical_not(full))):
        run = functools.partial(
            backward_step, per, at, list_ref, live_ref, geo_ref, kept_ref, ups, first_ref, second_ref, scratch
        )
        pl.when(within & chosen)(run)

    if begun:

        @pl.when(step == pl.num_programs(0) - 1)
        def _():
            for fetch in fetches:
                fetch.wait()
            tile_out[...] = (tile_acc[...] + fetched[2][...]).astype(BF)
            for n in range(9):
                row, cols = (8 - n) // 3, slice((8 - n) % 3 * CH, ((8 - n) % 3 + 1) * CH)
                for w, acc in enumerate((first_acc, second_acc)):
                    total = acc[row, :, cols] + fetched[w][row, :, cols]
                    kernels_out[w, n * CH : (n + 1) * CH] = (total * scale).astype(BF)


def backward(slot, plan, geo, kept, arrived, turned, sums, scale):
    steps, slots, live = plan
    readers = arrived.shape[0]
    begun = sums is not None
    whole = lambda *shape: pl.BlockSpec(shape, lambda i, *_: (0,) * len(shape))
    last = slots.shape[0] // PER - 1

    def group(i, n):
        return jnp.clip(base(slot, n) + jnp.minimum(i, n[1 + slot] - 1), 0, last)

    def from_reader(j):
        def block(i, n, s, *_):
            return jnp.clip(s[PER * group(i, n) + j] - 1 - slot * readers, 0, readers - 1), 0, 0

        return pl.BlockSpec((1, PACK, CH), block)

    totals = [(3, CH, WIDE), (3, CH, WIDE), (TH, TW, CH)]
    wide = [pltpu.VMEM((PER, FLAT + 2 * PITCH, WIDE), BF)] * 2
    if begun:
        outs = [jax.ShapeDtypeStruct((TH, TW, CH), BF), jax.ShapeDtypeStruct((2, 9 * CH, CH), BF)]
        scratch = wide + [pltpu.VMEM(t, F32) for t in totals] * 2 + [pltpu.SemaphoreType.DMA((3,))]
    else:
        outs = [jax.ShapeDtypeStruct(t, F32) for t in totals]
        scratch = wide
    return pl.pallas_call(
        functools.partial(backward_kernel, slot, begun, scale),
        grid_spec=pltpu.PrefetchScalarGridSpec(
            num_scalar_prefetch=4,
            grid=(readers // PER,),
            in_specs=[
                pl.BlockSpec((PER, 4, FLAT, CH), lambda i, n, *_: (group(i, n), 0, 0, 0)),
                *[from_reader(j) for j in range(PER)],
                whole(2, 9, CH, CH),
                *[pl.BlockSpec(memory_space=pl.ANY)] * (3 if begun else 0),
            ],
            out_specs=[whole(*o.shape) for o in outs],
            scratch_shapes=scratch,
        ),
        out_shape=outs,
        compiler_params=pltpu.CompilerParams(vmem_limit_bytes=VMEM),
    )(steps, slots, live, geo, kept, *[arrived] * PER, turned, *(sums or ()))


SIDE = 4
ORDERS = ((0, 1, 2), (1, 2, 0), (2, 0, 1))


def reduce_kernel(mine_ref, out_ref, pair_in, half, in_one, held_one, in_two, held_two, in_three, sems_s, sems_r):
    tile, line = lax.axis_index("tile"), lax.axis_index("group")
    core, x, z = tile & 1, (tile >> 1) & 3, tile >> 3
    coords = (z, x, line)
    third = mine_ref.shape[1] // 3
    quarter, small = third // SIDE, third // SIDE // SIDE

    def peer(axis, k):
        to = (coords[axis] + k) & (SIDE - 1)
        if axis == 0:
            return {"tile": to * 8 + x * 2 + core}
        if axis == 1:
            return {"tile": z * 8 + to * 2 + core}
        return {"group": to}

    other = {"tile": tile + 1 - 2 * core}

    def rows(start, size):
        return pl.ds(pl.multiple_of(start, 16), size)

    def remote(source, target, sem, device):
        return pltpu.make_async_remote_copy(
            source, target, sems_s.at[sem], sems_r.at[sem], device_id=device, device_id_type=MESH
        )

    barrier = pltpu.get_barrier_semaphore()
    pl.semaphore_signal(barrier, inc=1, device_id=other, device_id_type=MESH)
    for axis in range(3):
        for k in range(1, SIDE):
            pl.semaphore_signal(barrier, inc=1, device_id=peer(axis, k), device_id_type=MESH)
    pl.semaphore_wait(barrier, 1 + 3 * (SIDE - 1))

    def sem(stage, part, k):
        return 6 + (stage * 3 + part) * 3 + k - 1

    def swap(part):
        at = slice(part * third, (part + 1) * third)
        return remote(mine_ref.at[1 - core, at], pair_in.at[at], part, other)

    def one(part, k):
        axis = ORDERS[part][0]
        to = (coords[axis] + k) & (SIDE - 1)
        source = half.at[rows(part * third + to * quarter, quarter)]
        return remote(source, in_one.at[part, k - 1], sem(0, part, k), peer(axis, k))

    def two(part, k):
        axis = ORDERS[part][1]
        to = (coords[axis] + k) & (SIDE - 1)
        source = held_one.at[part, rows(to * small, small)]
        return remote(source, in_two.at[part, k - 1], sem(1, part, k), peer(axis, k))

    def three(part, k):
        return remote(held_two.at[part], in_three.at[part, k - 1], sem(2, part, k), peer(ORDERS[part][2], k))

    def start_of(part, first, second):
        return part * third + first * quarter + second * small

    def back_two(part, k, sender):
        first, second = ORDERS[part][:2]
        at = rows(start_of(part, coords[first], sender), small)
        return remote(out_ref.at[core, at], out_ref.at[core, at], sem(3, part, k), peer(second, k))

    def back_one(part, k, sender):
        first = ORDERS[part][0]
        at = rows(part * third + sender * quarter, quarter)
        return remote(out_ref.at[core, at], out_ref.at[core, at], sem(4, part, k), peer(first, k))

    def give(part, of):
        at = slice(part * third, (part + 1) * third)
        return remote(out_ref.at[of, at], out_ref.at[of, at], 3 + part, other)

    shifts = (2, 1, 3)
    parts = range(3)
    for part in parts:
        swap(part).start()
    for part in parts:
        swap(part).wait()
        at = slice(part * third, (part + 1) * third)
        half[at] = (mine_ref[core, at].astype(F32) + pair_in[at].astype(F32)).astype(BF)
        for k in shifts:
            one(part, k).start()
    for part in parts:
        own = coords[ORDERS[part][0]]
        total = half[rows(part * third + own * quarter, quarter)].astype(F32)
        for k in shifts:
            one(part, k).wait()
            total += in_one[part, k - 1].astype(F32)
        held_one[part] = total.astype(BF)
        for k in shifts:
            two(part, k).start()
    for part in parts:
        own = coords[ORDERS[part][1]]
        total = held_one[part, rows(own * small, small)].astype(F32)
        for k in shifts:
            two(part, k).wait()
            total += in_two[part, k - 1].astype(F32)
        held_two[part] = total.astype(BF)
        for k in shifts:
            three(part, k).start()
    for part in parts:
        first, second, axis = ORDERS[part]
        terms = {0: held_two[part].astype(F32)}
        for k in shifts:
            three(part, k).wait()
            terms[k] = in_three[part, k - 1].astype(F32)
        total = None
        for place in range(SIDE):
            back = (coords[axis] - place) & (SIDE - 1)
            term = terms[0]
            for k in shifts:
                term = jnp.where(back == k, terms[k], term)
            total = term if total is None else total + term
        out_ref[core, rows(start_of(part, coords[first], coords[second]), small)] = total.astype(BF)
        for k in shifts:
            back_two(part, k, coords[second]).start()
    for part in parts:
        first, second, axis = ORDERS[part]
        for k in shifts:
            back_two(part, k, coords[second]).wait_send()
            back_two(part, k, (coords[second] - k) & (SIDE - 1)).wait_recv()
        for k in shifts:
            back_one(part, k, coords[first]).start()
    for part in parts:
        first = ORDERS[part][0]
        for k in shifts:
            back_one(part, k, coords[first]).wait_send()
            back_one(part, k, (coords[first] - k) & (SIDE - 1)).wait_recv()
        give(part, core).start()
    for part in parts:
        give(part, core).wait_send()
        give(part, 1 - core).wait_recv()


def reduce_everywhere(mine):
    rows = mine.shape[1]
    third = rows // 3
    quarter, small = third // SIDE, third // SIDE // SIDE
    spec = pl.BlockSpec(memory_space=pltpu.VMEM)
    return pl.pallas_call(
        reduce_kernel,
        in_specs=[spec],
        out_specs=spec,
        out_shape=jax.ShapeDtypeStruct(mine.shape, BF),
        scratch_shapes=[
            pltpu.VMEM((rows, CH), BF),
            pltpu.VMEM((rows, CH), BF),
            pltpu.VMEM((3, SIDE - 1, quarter, CH), BF),
            pltpu.VMEM((3, quarter, CH), BF),
            pltpu.VMEM((3, SIDE - 1, small, CH), BF),
            pltpu.VMEM((3, small, CH), BF),
            pltpu.VMEM((3, SIDE - 1, small, CH), BF),
            pltpu.SemaphoreType.DMA((6 + 45,)),
            pltpu.SemaphoreType.DMA((6 + 45,)),
        ],
        compiler_params=pltpu.CompilerParams(
            collective_id=0, has_side_effects=True, vmem_limit_bytes=VMEM
        ),
    )(mine)


def send_plan(column, regions):
    owners = column.shape[0]
    ids = jnp.arange(owners, dtype=jnp.int32)
    before = jnp.sum(jnp.where(ids[None, :] < ids[:, None], column[None, :], 0), axis=1)
    k = jnp.arange(regions, dtype=jnp.int32)[:, None]
    mine = (before[None, :] <= k) & (k < (before + column)[None, :])
    slot = jnp.sum(jnp.where(mine, k - before[None, :], 0), axis=1, dtype=jnp.int32)
    owner = jnp.sum(jnp.where(mine, ids[None, :], 0), axis=1, dtype=jnp.int32)
    return slot, owner


def work_plan(row):
    readers = row.shape[0]
    ids = jnp.arange(readers, dtype=jnp.int32)
    place = jnp.arange(2 * readers, dtype=jnp.int32)[:, None]
    steps_zero = (jnp.sum(row > 0, dtype=jnp.int32) + PER - 1) // PER
    steps_one = (jnp.sum(row > 1, dtype=jnp.int32) + PER - 1) // PER
    slots = 0
    for s, start in ((0, 0), (1, PER * steps_zero)):
        has = row > s
        rank = jnp.sum(jnp.where((ids[None, :] < ids[:, None]) & has[None, :], 1, 0), axis=1)
        hit = has[None, :] & (start + rank[None, :] == place)
        slots += jnp.sum(jnp.where(hit, s * readers + ids[None, :] + 1, 0), axis=1, dtype=jnp.int32)
    return slots, jnp.stack([jnp.maximum(steps_zero + steps_one, 1), steps_zero, steps_one])


def exchange(blocks):
    return lax.all_to_all(blocks, "tile", split_axis=0, concat_axis=0, tiled=True)


def on_device(features, out_grad, pair_count, sample_grid, first_kernel, second_kernel):
    tiles, lines = lax.axis_size("tile"), lax.axis_size("group")
    own = lax.axis_index("tile")
    counts = pair_count[0]
    upstream = out_grad[0]
    regions = upstream.shape[0]
    column = lax.dynamic_index_in_dim(counts, own, 1, keepdims=False)
    row = lax.dynamic_index_in_dim(counts, own, 0, keepdims=False)

    packed = pack_upstream(send_plan(column, regions), upstream, tiles)
    arrived = [exchange(packed[0])]

    grid = jnp.swapaxes(sample_grid[0, 0], 0, 1).reshape(2 * tiles, 4, RES)
    row_at = 16 * grid[:, 0, 0:2] + grid[:, 1, 0:2]
    col_at = 16 * grid[:, 2, 0:2] + grid[:, 3, 0:2]
    geo = jnp.stack(
        [row_at[:, 0], row_at[:, 1] - row_at[:, 0], col_at[:, 0], col_at[:, 1] - col_at[:, 0]],
        axis=1,
    ).reshape(-1)
    slots, steps = work_plan(row)
    first, second = first_kernel.reshape(9, CH, CH), second_kernel.reshape(9, CH, CH)
    kept, turned = forward(steps, slots, slots, geo, features[0], first, second)
    later, kept = lax.optimization_barrier((packed[1], kept))
    arrived.append(exchange(later))
    scale = 1.0 / math.sqrt(lines * tiles * regions * RES * RES)
    sums = backward(0, (steps, slots, slots), geo, kept, arrived[0], turned, None, scale)
    tile_grad, parts = backward(1, (steps, slots, slots), geo, kept, arrived[1], turned, sums, scale)
    totals = reduce_everywhere(parts).astype(F32).reshape(2, 3, 3, CH, CH)
    return tile_grad[None], totals[0], totals[1]


def solution(mesh):
    return jax.shard_map(
        on_device,
        mesh=mesh,
        in_specs=(
            P("group", "tile", None, None),
            P("group", "tile", None, None, None),
            P("group", None, None),
            P("group", "tile", None, None, None, None),
            P(),
            P(),
        ),
        out_specs=(P("group", "tile", None, None), P(), P()),
        check_vma=False,
    )
```
